768 devices in a mesh: ty: 16 (over x, y_lo), tx: 48 (over z, y_hi, core).
Axes of the slice: x: 4, y: 8 (y_hi: 2, y_lo: 4; y = y_hi * 4 + y_lo), z: 12, core: 2. Of those that a mesh axis runs over, the one named last changes fastest.
Arguments:
- transmission: float32 [2, 2, 1024, 3072], P(None, None, 'ty', 'tx'), may hold values from -4 to 4
- probe_field: float32 [2, 128, 128], replicated, may hold values from -4 to 4
- propagator_phase: float32 [128, 128], replicated, may hold values from -3.140625 to 3.140625
- scan_offsets: int32 [16, 48, 6, 2], P('ty', 'tx'), may hold values from 0 to 64, as said below
- position_counts: int32 [16, 48], P('ty', 'tx'), may hold values from 1 to 6, as said below
- intensities: float32 [16, 48, 6, 128, 128], P('ty', 'tx'), may hold values from 0 to 2
Outputs:
- updated_object: float32 [2, 2, 1024, 3072], P(None, None, 'ty', 'tx')
The draws below stay inside these ranges and needn't reach their ends.
Inputs may be any that keep to these rules, and one draw needn't show every extreme that they name: `scan_offsets`: each pair is a row and a column offset within the extended region of 192 pixels; offsets 0 and 64 both occur. `position_counts`: positions k of a tile with k >= its count are ignored; some tile has 6 and some tile has 1.
All inputs are finite; a program needn't handle non-finite values.
Results may differ from the reference program's by a relative error of at most 0.0003.
Values sent between devices are 32-bit elements; how exact they have to be, the bound alone decides.
A program may use at most 32 MiB of HBM per device.

```python
import jax
import jax.numpy as jnp
from jax import lax

PROBE = 128
SLICES = 2
KPOS = 6
ITERS = 2
TY_TILES = 16
TX_TILES = 48
NY = 1024
NX = 3072


def draw_scan_offsets(key, part):
    base = jax.random.randint(key, (TY_TILES, TX_TILES, KPOS, 2), 0, PROBE // 2 + 1)
    base = base.at[0, 0, 0, 0].set(PROBE // 2)
    base = base.at[0, 0, 1, 1].set(0)
    return base.astype(jnp.int32)


def draw_position_counts(key, part):
    total = TY_TILES * TX_TILES
    flat = jax.random.randint(jax.random.fold_in(key, 11), (total,), 1, KPOS + 1)
    chosen = jax.random.randint(jax.random.fold_in(key, 12), (), 0, total)
    index = jnp.arange(total, dtype=jnp.int32)
    flat = jnp.where(index == chosen, KPOS, flat)
    flat = jnp.where(index == (chosen + 1) % total, 1, flat)
    return flat.reshape(TY_TILES, TX_TILES).astype(jnp.int32)


def block_scale(rng, dims, pieces, smallest, high):
    level, own = 1.0, jax.random.fold_in(rng, 6)
    for dim, shards_of in pieces:
        draws = jnp.exp(jax.random.uniform(jax.random.fold_in(own, dim), (shards_of,), jnp.float32, smallest / len(pieces), high / len(pieces)))
        level = level * jnp.repeat(draws, dims[dim] // shards_of).reshape([-1 if axis == dim else 1 for axis in range(len(dims))])
    return level


def scatter_about(stream_key, dims, scale, bound, split=(), held_as=jnp.bfloat16):
    result = jax.random.normal(stream_key, dims, jnp.float32) * scale
    if len(split) > 0:
        result = block_scale(stream_key, dims, split, -0.22, 0.18) * result
    return jnp.clip(result, min=-bound, max=bound).astype(held_as)


def setup_inputs(seed: int = 0) -> dict:
    streams_of = jax.random.split(jax.random.key(seed), 7)
    return {
        "transmission": scatter_about(streams_of[0], (2, SLICES, NY, NX), 0.7, 4.0, ((2, 16), (3, 48)), jnp.float32),
        "probe_field": scatter_about(streams_of[1], (2, PROBE, PROBE), 0.7, 4.0, (), jnp.float32),
        "propagator_phase": jnp.clip(jax.random.uniform(streams_of[2], (PROBE, PROBE), jnp.float32, -3.140625, 3.140625), -3.140625, 3.140625),
        "scan_offsets": draw_scan_offsets(jax.random.fold_in(streams_of[6], 71), 0),
        "position_counts": draw_position_counts(jax.random.fold_in(streams_of[6], 71), 0),
        "intensities": jnp.clip(2.0 * jax.random.uniform(streams_of[5], (TY_TILES, TX_TILES, KPOS, PROBE, PROBE), jnp.float32) ** block_scale(streams_of[5], (TY_TILES, TX_TILES, KPOS, PROBE, PROBE), ((0, 16), (1, 48)), -0.2, 0.2), 0.0, 2.0),
    }


def tile_loss(extended, probe_field, propagator, offsets, active, measured):
    size = probe_field.shape[1]
    layers = extended.shape[1]
    zero_index = jnp.zeros((), jnp.int32)

    def window(offset):
        return lax.dynamic_slice(extended, (zero_index, zero_index, offset[0].astype(jnp.int32), offset[1].astype(jnp.int32)), (2, layers, size, size))
    windows = jax.vmap(window)(offsets)
    field = (probe_field[0] + 1j * probe_field[1])[None]
    for layer in range(layers):
        slice_field = windows[:, 0, layer] + 1j * windows[:, 1, layer]
        field = field * slice_field
        if layer < layers - 1:
            field = jnp.fft.ifft2(propagator[None] * jnp.fft.fft2(field, norm='ortho'), norm='ortho')
    far_field = jnp.fft.fft2(field, norm='ortho')
    power = jnp.real(far_field) ** 2 + jnp.imag(far_field) ** 2
    return jnp.sum(active[:, None, None] * (power - measured) ** 2)

def reference(transmission, probe_field, propagator_phase, scan_offsets, position_counts, intensities):
    core = PROBE // 2
    layers = transmission.shape[1]
    propagator = jnp.cos(propagator_phase) + 1j * jnp.sin(propagator_phase)
    slots = jnp.arange(KPOS, dtype=jnp.int32)
    tiles = jnp.arange(TY_TILES * TX_TILES, dtype=jnp.int32)
    zero_index = jnp.zeros((), jnp.int32)
    current = transmission
    for sweep in range(ITERS):
        padded = jnp.pad(current, ((0, 0), (0, 0), (core, core), (core, core)))

        def visit(total, tile):
            row_index = (tile // TX_TILES).astype(jnp.int32)
            col_index = (tile % TX_TILES).astype(jnp.int32)
            start = (zero_index, zero_index, row_index * core, col_index * core)
            extended = lax.dynamic_slice(padded, start, (2, layers, 3 * core, 3 * core))
            active = (slots < position_counts[row_index, col_index]).astype(jnp.float32)
            grad_tile = jax.grad(tile_loss)(extended, probe_field, propagator, scan_offsets[row_index, col_index], active, intensities[row_index, col_index])
            region = lax.dynamic_slice(total, start, (2, layers, 3 * core, 3 * core))
            return (lax.dynamic_update_slice(total, region + grad_tile, start), None)
        summed, unused = lax.scan(visit, jnp.zeros(padded.shape, jnp.float32), tiles)
        current = current - 0.003 * summed[:, :, core:-core, core:-core]
    return current
```

```python
import functools
import math

import jax
import jax.numpy as jnp
import numpy as np
from jax import lax
from jax.experimental import pallas as pl
from jax.experimental.pallas import tpu as pltpu
from jax.sharding import PartitionSpec as P

ITERS = 2
STEP = 0.003
SIZE = 128
CORE = 64
SLOTS = 6
F32 = jnp.float32
BF16 = jnp.bfloat16

UP, DOWN, OUT, PAIR, OUT_UP, OUT_DOWN, PAIR_UP, PAIR_DOWN = range(8)
ROW_UP, ROW_DOWN, ROW_OWN = range(3)
ROW_START = (0, 128, 64)
COL_OUT, COL_OWN, COL_PAIR = range(3)
ADD_PAIR, CORNER_UP, CORNER_DOWN, ADD_UP, ADD_DOWN, ADD_OUT = range(6)
COPIES = 14


def dft_blocks():
    index = np.arange(SIZE)
    angle = 2.0 * math.pi / SIZE * ((index[:, None] * index[None, :]) % SIZE)
    re = np.cos(angle) / math.sqrt(SIZE)
    im = -np.sin(angle) / math.sqrt(SIZE)
    right = np.block([[re, im], [-im, re]])
    blocks = np.stack([right, right.T])
    high = blocks.astype(BF16)
    low = (blocks - high.astype(np.float64)).astype(BF16)
    return np.stack([high, low], axis=1)


def split(x):
    high = x.astype(BF16)
    return high, (x - high.astype(F32)).astype(BF16)


def dot(a, b):
    return jnp.dot(a, b, preferred_element_type=F32)


def from_right(fields, table):
    high, low = split(
        jnp.concatenate(
            [
                jnp.concatenate([fields[0], fields[1]], axis=1),
                jnp.concatenate([fields[2], fields[3]], axis=1),
            ],
            axis=0,
        )
    )
    out = dot(high, table[0]) + dot(low, table[0]) + dot(high, table[1])
    return out[:SIZE, :SIZE], out[:SIZE, SIZE:], out[SIZE:, :SIZE], out[SIZE:, SIZE:]


def from_left(fields, table):
    high, low = split(
        jnp.concatenate(
            [
                jnp.concatenate([fields[0], fields[2]], axis=1),
                jnp.concatenate([fields[1], fields[3]], axis=1),
            ],
            axis=0,
        )
    )
    out = dot(table[0], high) + dot(table[0], low) + dot(table[1], high)
    return out[:SIZE, :SIZE], out[SIZE:, :SIZE], out[:SIZE, SIZE:], out[SIZE:, SIZE:]


def times(a, b):
    return a[0] * b[0] - a[1] * b[1], a[0] * b[1] + a[1] * b[0]


def times_conj(a, b):
    return a[0] * b[0] + a[1] * b[1], a[1] * b[0] - a[0] * b[1]


def lanes_of(shape):
    return lax.broadcasted_iota(jnp.int32, shape, 1)


def load_window(ext, offs, slice_, slot):
    row, col = offs[0, 0, slot, 0], offs[0, 0, slot, 1]
    rows = pl.ds(row, SIZE)
    back = lax.rem(SIZE - col, SIZE)
    keep = lanes_of((SIZE, SIZE)) < SIZE - col
    last = ext[slice_, 2, rows, :]
    re = jnp.where(
        keep, pltpu.roll(ext[slice_, 0, rows, :], back, 1), pltpu.roll(last, back, 1)
    )
    im = jnp.where(
        keep, pltpu.roll(ext[slice_, 1, rows, :], back, 1), pltpu.roll(last, CORE - col, 1)
    )
    return re, im


def store_field(padded, offs, slot, field):
    col = offs[0, 0, slot, 1]
    for part in range(2):
        padded[slot, part, CORE : CORE + SIZE, :] = pltpu.roll(field[part], col, 1)


def gradient_rows(padded, offs, start):
    lane = lanes_of((CORE, SIZE))
    sums = [jnp.zeros((CORE, SIZE), F32) for _ in range(4)]
    for slot in range(SLOTS):
        row, col = offs[0, 0, slot, 0], offs[0, 0, slot, 1]
        rows = pl.ds(CORE + start - row, CORE)
        here = lane >= col
        for part in range(2):
            value = padded[slot, part, rows, :]
            sums[part] = sums[part] + jnp.where(here, value, 0.0)
            sums[2 + part] = sums[2 + part] + jnp.where(here, 0.0, value)
    low = lane < CORE
    first = jnp.where(low, sums[0], pltpu.roll(sums[1], CORE, 1))
    second = jnp.where(low, pltpu.roll(sums[0], CORE, 1), sums[1])
    third = jnp.where(low, sums[2], pltpu.roll(sums[3], CORE, 1))
    return first, second, third


def forward_first(ext, offs, probe, prop, tables, psi):
    for pair in range(SLOTS // 2):
        fields = ()
        for slot in (2 * pair, 2 * pair + 1):
            fields += times(
                (probe[0], probe[1]), load_window(ext, offs, 0, slot)
            )
        fields = from_right(fields, tables[0])
        fields = from_left(fields, tables[1])
        factor = (prop[0], prop[1])
        fields = times(fields[:2], factor) + times(fields[2:], factor)
        fields = from_left(fields, tables[0])
        fields = from_right(fields, tables[1])
        for n in range(2):
            for part in range(2):
                psi[2 * pair + n, part] = fields[2 * n + part]


def middle(ext, offs, counts, measured, tables, psi, back, padded):
    for pair in range(SLOTS // 2):
        slots = (2 * pair, 2 * pair + 1)
        windows, fields = [], ()
        for slot in slots:
            window = load_window(ext, offs, 1, slot)
            windows.append(window)
            fields += times((psi[slot, 0], psi[slot, 1]), window)
        fields = from_right(fields, tables[0])
        fields = from_left(fields, tables[1])
        grads = ()
        for n, slot in enumerate(slots):
            re, im = fields[2 * n], fields[2 * n + 1]
            live = jnp.where(slot < counts[0, 0], 4.0, 0.0)
            factor = live * (re * re + im * im - measured[0, 0, slot])
            grads += (factor * re, factor * im)
        grads = from_left(grads, tables[0])
        grads = from_right(grads, tables[1])
        for n, slot in enumerate(slots):
            grad = grads[2 * n : 2 * n + 2]
            field = times_conj(grad, windows[n])
            for part in range(2):
                back[slot, part] = field[part]
            store_field(
                padded, offs, slot, times_conj(grad, (psi[slot, 0], psi[slot, 1]))
            )


def backward_first(offs, probe, prop, tables, back, padded):
    for pair in range(SLOTS // 2):
        slots = (2 * pair, 2 * pair + 1)
        fields = ()
        for slot in slots:
            fields += (back[slot, 0], back[slot, 1])
        fields = from_right(fields, tables[0])
        fields = from_left(fields, tables[1])
        factor = (prop[0], prop[1])
        fields = times_conj(fields[:2], factor) + times_conj(fields[2:], factor)
        fields = from_left(fields, tables[0])
        fields = from_right(fields, tables[1])
        for n, slot in enumerate(slots):
            store_field(
                padded,
                offs,
                slot,
                times_conj(fields[2 * n : 2 * n + 2], (probe[0], probe[1])),
            )


def kernel(
    mesh_shape,
    obj,
    probe,
    phase,
    offs,
    counts,
    measured,
    tables,
    out,
    own,
    halo,
    grads,
    passed,
    added,
    ext,
    prop,
    psi,
    back,
    padded,
    send_sems,
    recv_sems,
):
    ty_count, tx_count = mesh_shape
    row, col = lax.axis_index("ty"), lax.axis_index("tx")
    even = lax.rem(col, 2) == 0
    above = {"ty": lax.rem(row + ty_count - 1, ty_count)}
    below = {"ty": lax.rem(row + 1, ty_count)}
    right = lax.rem(col + 1, tx_count)
    left = lax.rem(col + tx_count - 1, tx_count)
    outer = {"tx": jnp.where(even, left, right)}
    partner = {"tx": jnp.where(even, right, left)}
    has_above = row > 0
    has_below = row < ty_count - 1
    has_outer = jnp.logical_and(col > 0, col < tx_count - 1)

    barrier = pltpu.get_barrier_semaphore()
    for target in (above, below, outer, partner):
        pl.semaphore_signal(
            barrier, inc=1, device_id=target, device_id_type=pl.DeviceIdType.MESH
        )

    low = lanes_of((CORE, SIZE)) < CORE
    for s in range(2):
        re = jnp.concatenate([obj[0, s], obj[1, s]], axis=1)
        own[0, s] = re
    pl.semaphore_wait(barrier, 4)

    started = []

    def send(src, dst, step, s, kind, target):
        copy = pltpu.make_async_remote_copy(
            src_ref=src,
            dst_ref=dst,
            send_sem=send_sems.at[step, s, kind],
            recv_sem=recv_sems.at[step, s, kind],
            device_id=target,
            device_id_type=pl.DeviceIdType.MESH,
        )
        copy.start()
        started.append(copy)
        return copy

    def send_halo(step, s, kind, src, target):
        return send(src, halo.at[step, s, kind], step, s, kind, target)

    def halo_first(step, s):
        mine = own.at[step, s]
        return {
            OUT: send_halo(step, s, OUT, mine, outer),
            DOWN: send_halo(step, s, DOWN, mine, above),
            UP: send_halo(step, s, UP, mine, below),
            PAIR: send_halo(step, s, PAIR, mine, partner),
        }

    def halo_second(step, s, copies):
        copies[OUT].wait_recv()
        copies[OUT_DOWN] = send_halo(step, s, OUT_DOWN, halo.at[step, s, OUT], above)
        copies[OUT_UP] = send_halo(step, s, OUT_UP, halo.at[step, s, OUT], below)
        copies[UP].wait_recv()
        copies[PAIR_UP] = send_halo(step, s, PAIR_UP, halo.at[step, s, UP], partner)
        copies[DOWN].wait_recv()
        copies[PAIR_DOWN] = send_halo(
            step, s, PAIR_DOWN, halo.at[step, s, DOWN], partner
        )

    def place(s, start, out_tile, own_tile, pair_tile):
        first = jnp.where(even, out_tile, pair_tile)
        third = jnp.where(even, pair_tile, out_tile)
        rows = slice(start, start + CORE)
        ext[s, 0, rows, :] = jnp.where(low, first, pltpu.roll(own_tile, CORE, 1))
        ext[s, 1, rows, :] = jnp.where(low, pltpu.roll(first, CORE, 1), own_tile)
        ext[s, 2, rows, :] = third

    def halo_last(step, s, copies):
        for kind in (PAIR, OUT_UP, PAIR_UP, OUT_DOWN, PAIR_DOWN):
            copies[kind].wait_recv()
        tile = lambda kind, ok: jnp.where(ok, halo[step, s, kind], 0.0)
        both = jnp.logical_and
        place(s, CORE, tile(OUT, has_outer), own[step, s], halo[step, s, PAIR])
        place(
            s,
            0,
            tile(OUT_UP, both(has_outer, has_above)),
            tile(UP, has_above),
            tile(PAIR_UP, has_above),
        )
        place(
            s,
            2 * CORE,
            tile(OUT_DOWN, both(has_outer, has_below)),
            tile(DOWN, has_below),
            tile(PAIR_DOWN, has_below),
        )

    def reduce_first(step, s):
        for tile in (ROW_UP, ROW_DOWN, ROW_OWN):
            first, second, third = gradient_rows(padded.at[s], offs, ROW_START[tile])
            grads[step, s, COL_PAIR, tile] = jnp.where(even, third, first)
            grads[step, s, COL_OUT, tile] = jnp.where(even, first, third)
            grads[step, s, COL_OWN, tile] = second
        sent = grads.at[step, s]
        return {
            CORNER_DOWN: send(
                sent.at[COL_OUT, ROW_UP],
                added.at[step, s, CORNER_DOWN - 1],
                step,
                s,
                8 + CORNER_DOWN,
                above,
            ),
            CORNER_UP: send(
                sent.at[COL_OUT, ROW_DOWN],
                added.at[step, s, CORNER_UP - 1],
                step,
                s,
                8 + CORNER_UP,
                below,
            ),
            ADD_PAIR: send(
                sent.at[COL_PAIR], passed.at[step, s], step, s, 8 + ADD_PAIR, partner
            ),
        }

    def masked(step, s, kind, ok):
        return jnp.where(ok, added[step, s, kind - 1], 0.0)

    def reduce_second(step, s, copies):
        mine = grads.at[step, s]

        def pass_on(kind, src, target):
            copies[kind] = send(
                src, added.at[step, s, kind - 1], step, s, 8 + kind, target
            )

        copies[ADD_PAIR].wait_recv()
        for tile, kind, target in ((ROW_UP, ADD_DOWN, above), (ROW_DOWN, ADD_UP, below)):
            mine[COL_OWN, tile] = mine[COL_OWN, tile] + passed[step, s, tile]
            pass_on(kind, mine.at[COL_OWN, tile], target)
        copies[CORNER_UP].wait_recv()
        copies[CORNER_DOWN].wait_recv()
        mine[COL_OUT, ROW_OWN] = (
            mine[COL_OUT, ROW_OWN]
            + masked(step, s, CORNER_UP, has_above)
            + masked(step, s, CORNER_DOWN, has_below)
        )
        pass_on(ADD_OUT, mine.at[COL_OUT, ROW_OWN], outer)

    def reduce_last(step, s, copies):
        total = grads[step, s, COL_OWN, ROW_OWN] + passed[step, s, ROW_OWN]
        for kind, ok in ((ADD_UP, has_above), (ADD_DOWN, has_below), (ADD_OUT, has_outer)):
            copies[kind].wait_recv()
            total = total + masked(step, s, kind, ok)
        return own[step, s] - STEP * total

    first0 = halo_first(0, 0)
    first1 = halo_first(0, 1)
    prop[0] = jnp.cos(phase[...])
    prop[1] = jnp.sin(phase[...])
    zero = jnp.zeros((CORE, SIZE), F32)
    for s in range(2):
        for slot in range(SLOTS):
            for part in range(2):
                padded[s, slot, part, :CORE, :] = zero
                padded[s, slot, part, CORE + SIZE :, :] = zero

    for step in range(ITERS):
        halo_second(step, 0, first0)
        halo_second(step, 1, first1)
        halo_last(step, 0, first0)
        forward_first(ext, offs, probe, prop, tables, psi)
        halo_last(step, 1, first1)
        middle(ext, offs, counts, measured, tables, psi, back, padded.at[1])
        sums1 = reduce_first(step, 1)
        backward_first(offs, probe, prop, tables, back, padded.at[0])
        reduce_second(step, 1, sums1)
        sums0 = reduce_first(step, 0)
        reduce_second(step, 0, sums0)
        for s, sums in ((0, sums0), (1, sums1)):
            new = reduce_last(step, s, sums)
            if step < ITERS - 1:
                own[step + 1, s] = new
                copies = halo_first(step + 1, s)
                if s == 0:
                    first0 = copies
                else:
                    first1 = copies
            else:
                out[0, s] = new[:, :CORE]
                out[1, s] = pltpu.roll(new, CORE, 1)[:, :CORE]
    for copy in started:
        copy.wait_send()


def solution(mesh):
    shape = (mesh.shape["ty"], mesh.shape["tx"])
    vmem = pl.BlockSpec(memory_space=pltpu.VMEM)
    smem = pl.BlockSpec(memory_space=pltpu.SMEM)
    tables = dft_blocks()

    def on_device(
        transmission, probe_field, propagator_phase, scan_offsets, position_counts, intensities
    ):
        tile = (CORE, SIZE)
        field = (SIZE, SIZE)
        return pl.pallas_call(
            functools.partial(kernel, shape),
            out_shape=jax.ShapeDtypeStruct(transmission.shape, F32),
            in_specs=[vmem, vmem, vmem, smem, smem, vmem, vmem],
            out_specs=vmem,
            scratch_shapes=[
                pltpu.VMEM((ITERS, 2) + tile, F32),
                pltpu.VMEM((ITERS, 2, 8) + tile, F32),
                pltpu.VMEM((ITERS, 2, 3, 3) + tile, F32),
                pltpu.VMEM((ITERS, 2, 3) + tile, F32),
                pltpu.VMEM((ITERS, 2, 5) + tile, F32),
                pltpu.VMEM((2, 3, 3 * CORE, SIZE), F32),
                pltpu.VMEM((2,) + field, F32),
                pltpu.VMEM((SLOTS, 2) + field, F32),
                pltpu.VMEM((SLOTS, 2) + field, F32),
                pltpu.VMEM((2, SLOTS, 2, 2 * SIZE, SIZE), F32),
                pltpu.SemaphoreType.DMA((ITERS, 2, COPIES)),
                pltpu.SemaphoreType.DMA((ITERS, 2, COPIES)),
            ],
            compiler_params=pltpu.CompilerParams(
                collective_id=0, has_side_effects=True, vmem_limit_bytes=48 * 1024 * 1024
            ),
        )(
            transmission,
            probe_field,
            propagator_phase,
            scan_offsets,
            position_counts,
            intensities,
            jnp.asarray(tables),
        )

    return jax.shard_map(
        on_device,
        mesh=mesh,
        in_specs=(
            P(None, None, "ty", "tx"),
            P(),
            P(),
            P("ty", "tx", None, None),
            P("ty", "tx"),
            P("ty", "tx", None, None, None),
        ),
        out_specs=P(None, None, "ty", "tx"),
        check_vma=False,
    )
```

```python
import functools
import math

import jax
import jax.numpy as jnp
import numpy as np
from jax import lax
from jax.experimental import pallas as pl
from jax.experimental.pallas import tpu as pltpu
from jax.sharding import PartitionSpec as P

ITERS = 2
STEP = 0.003
SIZE = 128
CORE = 64
SLOTS = 6
F32 = jnp.float32
BF16 = jnp.bfloat16

UP, DOWN, OUT, PAIR, OUT_UP, OUT_DOWN, PAIR_UP, PAIR_DOWN = range(8)
ROW_UP, ROW_DOWN, ROW_OWN = range(3)
ROW_START = (0, 128, 64)
COL_OUT, COL_OWN, COL_PAIR = range(3)
ADD_PAIR, CORNER_UP, CORNER_DOWN, ADD_UP, ADD_DOWN, ADD_OUT = range(6)
COPIES = 14


def dft_blocks():
    index = np.arange(SIZE)
    angle = 2.0 * math.pi / SIZE * ((index[:, None] * index[None, :]) % SIZE)
    re = np.cos(angle) / math.sqrt(SIZE)
    im = -np.sin(angle) / math.sqrt(SIZE)
    right = np.block([[re, im], [-im, re]])
    blocks = np.stack([right, right.T])
    high = blocks.astype(BF16)
    low = (blocks - high.astype(np.float64)).astype(BF16)
    return np.stack([high, low], axis=1)


def split(x):
    high = x.astype(BF16)
    return high, (x - high.astype(F32)).astype(BF16)


def dot(a, b):
    return jnp.dot(a, b, preferred_element_type=F32)


def from_right(fields, table):
    high, low = split(
        jnp.concatenate(
            [
                jnp.concatenate([fields[0], fields[1]], axis=1),
                jnp.concatenate([fields[2], fields[3]], axis=1),
            ],
            axis=0,
        )
    )
    out = dot(high, table[0]) + dot(low, table[0]) + dot(high, table[1])
    return out[:SIZE, :SIZE], out[:SIZE, SIZE:], out[SIZE:, :SIZE], out[SIZE:, SIZE:]


def from_left(fields, table):
    high, low = split(
        jnp.concatenate(
            [
                jnp.concatenate([fields[0], fields[2]], axis=1),
                jnp.concatenate([fields[1], fields[3]], axis=1),
            ],
            axis=0,
        )
    )
    out = dot(table[0], high) + dot(table[0], low) + dot(table[1], high)
    return out[:SIZE, :SIZE], out[SIZE:, :SIZE], out[:SIZE, SIZE:], out[SIZE:, SIZE:]


def times(a, b):
    return a[0] * b[0] - a[1] * b[1], a[0] * b[1] + a[1] * b[0]


def times_conj(a, b):
    return a[0] * b[0] + a[1] * b[1], a[1] * b[0] - a[0] * b[1]


def lanes_of(shape):
    return lax.broadcasted_iota(jnp.int32, shape, 1)


def load_window(ext, offs, slice_, slot):
    row, col = offs[0, 0, 0, slot], offs[0, 0, 1, slot]
    rows = pl.ds(row, SIZE)
    back = lax.rem(SIZE - col, SIZE)
    keep = lanes_of((SIZE, SIZE)) < SIZE - col
    last = ext[slice_, 2, rows, :]
    re = jnp.where(
        keep, pltpu.roll(ext[slice_, 0, rows, :], back, 1), pltpu.roll(last, back, 1)
    )
    im = jnp.where(
        keep, pltpu.roll(ext[slice_, 1, rows, :], back, 1), pltpu.roll(last, CORE - col, 1)
    )
    return re, im


def store_field(padded, offs, slot, field):
    col = offs[0, 0, 1, slot]
    for part in range(2):
        padded[slot, part, CORE : CORE + SIZE, :] = pltpu.roll(field[part], col, 1)


def gradient_rows(padded, offs, start):
    lane = lanes_of((CORE, SIZE))
    sums = [jnp.zeros((CORE, SIZE), F32) for _ in range(4)]
    for slot in range(SLOTS):
        row, col = offs[0, 0, 0, slot], offs[0, 0, 1, slot]
        rows = pl.ds(CORE + start - row, CORE)
        here = lane >= col
        for part in range(2):
            value = padded[slot, part, rows, :]
            sums[part] = sums[part] + jnp.where(here, value, 0.0)
            sums[2 + part] = sums[2 + part] + jnp.where(here, 0.0, value)
    low = lane < CORE
    first = jnp.where(low, sums[0], pltpu.roll(sums[1], CORE, 1))
    second = jnp.where(low, pltpu.roll(sums[0], CORE, 1), sums[1])
    third = jnp.where(low, sums[2], pltpu.roll(sums[3], CORE, 1))
    return first, second, third


def forward_first(ext, offs, probe, prop, tables, psi):
    for pair in range(SLOTS // 2):
        fields = ()
        for slot in (2 * pair, 2 * pair + 1):
            fields += times(
                (probe[0], probe[1]), load_window(ext, offs, 0, slot)
            )
        fields = from_right(fields, tables[0])
        fields = from_left(fields, tables[1])
        factor = (prop[0], prop[1])
        fields = times(fields[:2], factor) + times(fields[2:], factor)
        fields = from_left(fields, tables[0])
        fields = from_right(fields, tables[1])
        for n in range(2):
            for part in range(2):
                psi[2 * pair + n, part] = fields[2 * n + part]


def middle(ext, offs, counts, measured, tables, psi, back, padded):
    for pair in range(SLOTS // 2):
        slots = (2 * pair, 2 * pair + 1)
        windows, fields = [], ()
        for slot in slots:
            window = load_window(ext, offs, 1, slot)
            windows.append(window)
            fields += times((psi[slot, 0], psi[slot, 1]), window)
        fields = from_right(fields, tables[0])
        fields = from_left(fields, tables[1])
        grads = ()
        for n, slot in enumerate(slots):
            re, im = fields[2 * n], fields[2 * n + 1]
            live = jnp.where(slot < counts[0, 0], 4.0, 0.0)
            factor = live * (re * re + im * im - measured[0, 0, slot])
            grads += (factor * re, factor * im)
        grads = from_left(grads, tables[0])
        grads = from_right(grads, tables[1])
        for n, slot in enumerate(slots):
            grad = grads[2 * n : 2 * n + 2]
            field = times_conj(grad, windows[n])
            for part in range(2):
                back[slot, part] = field[part]
            store_field(
                padded, offs, slot, times_conj(grad, (psi[slot, 0], psi[slot, 1]))
            )


def backward_first(offs, probe, prop, tables, back, padded):
    for pair in range(SLOTS // 2):
        slots = (2 * pair, 2 * pair + 1)
        fields = ()
        for slot in slots:
            fields += (back[slot, 0], back[slot, 1])
        fields = from_right(fields, tables[0])
        fields = from_left(fields, tables[1])
        factor = (prop[0], prop[1])
        fields = times_conj(fields[:2], factor) + times_conj(fields[2:], factor)
        fields = from_left(fields, tables[0])
        fields = from_right(fields, tables[1])
        for n, slot in enumerate(slots):
            store_field(
                padded,
                offs,
                slot,
                times_conj(fields[2 * n : 2 * n + 2], (probe[0], probe[1])),
            )


def kernel(
    mesh_shape,
    obj_in,
    probe_in,
    phase_in,
    offs_in,
    counts_in,
    measured_in,
    tables_in,
    out,
    obj,
    probe,
    phase,
    offs,
    counts,
    measured,
    tables,
    own,
    halo,
    grads,
    passed,
    added,
    ext,
    prop,
    psi,
    back,
    padded,
    send_sems,
    recv_sems,
    load_sems,
):
    ty_count, tx_count = mesh_shape
    row, col = lax.axis_index("ty"), lax.axis_index("tx")
    even = lax.rem(col, 2) == 0
    up = lax.rem(row + ty_count - 1, ty_count)
    down = lax.rem(row + 1, ty_count)
    right = lax.rem(col + 1, tx_count)
    left = lax.rem(col + tx_count - 1, tx_count)
    side = jnp.where(even, left, right)
    outer = {"ty": row, "tx": side}
    partner = {"ty": row, "tx": jnp.where(even, right, left)}
    above, below = {"ty": up, "tx": col}, {"ty": down, "tx": col}
    outer_above, outer_below = {"ty": up, "tx": side}, {"ty": down, "tx": side}
    has_above = row > 0
    has_below = row < ty_count - 1
    has_outer = jnp.logical_and(col > 0, col < tx_count - 1)

    barrier = pltpu.get_barrier_semaphore()
    for target in (outer, outer_above, outer_below, above, below, partner):
        pl.semaphore_signal(
            barrier, inc=1, device_id=target, device_id_type=pl.DeviceIdType.MESH
        )

    loads = [
        pltpu.make_async_copy(src, dst, load_sems.at[n])
        for n, (src, dst) in enumerate(
            (
                (obj_in, obj),
                (phase_in, phase),
                (offs_in, offs),
                (counts_in, counts),
                (probe_in, probe),
                (tables_in, tables),
                (measured_in, measured),
            )
        )
    ]
    for load in loads:
        load.start()

    low = lanes_of((CORE, SIZE)) < CORE
    loads[0].wait()
    for s in range(2):
        own[0, s] = jnp.concatenate([obj[0, s], obj[1, s]], axis=1)
    pl.semaphore_wait(barrier, 6)

    started = []

    def send(src, dst, step, s, kind, target):
        copy = pltpu.make_async_remote_copy(
            src_ref=src,
            dst_ref=dst,
            send_sem=send_sems.at[step, s, kind],
            recv_sem=recv_sems.at[step, s, kind],
            device_id=target,
            device_id_type=pl.DeviceIdType.MESH,
        )
        copy.start()
        started.append(copy)
        return copy

    def send_halo(step, s, kind, src, target):
        return send(src, halo.at[step, s, kind], step, s, kind, target)

    def halo_first(step, s):
        mine = own.at[step, s]
        return {
            kind: send_halo(step, s, kind, mine, target)
            for kind, target in (
                (OUT, outer),
                (OUT_DOWN, outer_above),
                (OUT_UP, outer_below),
                (DOWN, above),
                (UP, below),
                (PAIR, partner),
            )
        }

    def halo_second(step, s, copies):
        for kind, passed_on in ((UP, PAIR_UP), (DOWN, PAIR_DOWN)):
            copies[kind].wait_recv()
            copies[passed_on] = send_halo(
                step, s, passed_on, halo.at[step, s, kind], partner
            )

    def place(s, start, out_tile, own_tile, pair_tile):
        first = jnp.where(even, out_tile, pair_tile)
        third = jnp.where(even, pair_tile, out_tile)
        rows = slice(start, start + CORE)
        ext[s, 0, rows, :] = jnp.where(low, first, pltpu.roll(own_tile, CORE, 1))
        ext[s, 1, rows, :] = jnp.where(low, pltpu.roll(first, CORE, 1), own_tile)
        ext[s, 2, rows, :] = third

    def halo_last(step, s, copies):
        for kind in (PAIR, PAIR_UP, PAIR_DOWN, OUT_UP, OUT_DOWN, OUT):
            copies[kind].wait_recv()
        tile = lambda kind, ok: jnp.where(ok, halo[step, s, kind], 0.0)
        both = jnp.logical_and
        place(s, CORE, tile(OUT, has_outer), own[step, s], halo[step, s, PAIR])
        place(
            s,
            0,
            tile(OUT_UP, both(has_outer, has_above)),
            tile(UP, has_above),
            tile(PAIR_UP, has_above),
        )
        place(
            s,
            2 * CORE,
            tile(OUT_DOWN, both(has_outer, has_below)),
            tile(DOWN, has_below),
            tile(PAIR_DOWN, has_below),
        )

    def reduce_first(step, s):
        sent = grads.at[step, s]
        copies = {}
        for tile, kind, target in (
            (ROW_UP, CORNER_DOWN, outer_above),
            (ROW_DOWN, CORNER_UP, outer_below),
            (ROW_OWN, ADD_OUT, outer),
        ):
            first, second, third = gradient_rows(padded.at[s], offs, ROW_START[tile])
            sent[COL_OUT, tile] = jnp.where(even, first, third)
            copies[kind] = send(
                sent.at[COL_OUT, tile],
                added.at[step, s, kind - 1],
                step,
                s,
                8 + kind,
                target,
            )
            sent[COL_PAIR, tile] = jnp.where(even, third, first)
            sent[COL_OWN, tile] = second
        copies[ADD_PAIR] = send(
            sent.at[COL_PAIR], passed.at[step, s], step, s, 8 + ADD_PAIR, partner
        )
        return copies

    def masked(step, s, kind, ok):
        return jnp.where(ok, added[step, s, kind - 1], 0.0)

    def reduce_second(step, s, copies):
        mine = grads.at[step, s]
        copies[ADD_PAIR].wait_recv()
        for tile, kind, target in ((ROW_UP, ADD_DOWN, above), (ROW_DOWN, ADD_UP, below)):
            mine[COL_OWN, tile] = mine[COL_OWN, tile] + passed[step, s, tile]
            copies[kind] = send(
                mine.at[COL_OWN, tile],
                added.at[step, s, kind - 1],
                step,
                s,
                8 + kind,
                target,
            )

    def reduce_last(step, s, copies):
        total = grads[step, s, COL_OWN, ROW_OWN] + passed[step, s, ROW_OWN]
        both = jnp.logical_and
        for kind, ok in (
            (ADD_UP, has_above),
            (ADD_DOWN, has_below),
            (CORNER_UP, both(has_above, has_outer)),
            (CORNER_DOWN, both(has_below, has_outer)),
            (ADD_OUT, has_outer),
        ):
            copies[kind].wait_recv()
            total = total + masked(step, s, kind, ok)
        return own[step, s] - STEP * total

    first0 = halo_first(0, 0)
    first1 = halo_first(0, 1)
    loads[1].wait()
    prop[0] = jnp.cos(phase[...])
    prop[1] = jnp.sin(phase[...])
    zero = jnp.zeros((CORE, SIZE), F32)
    for s in range(2):
        for slot in range(SLOTS):
            for part in range(2):
                padded[s, slot, part, :CORE, :] = zero
                padded[s, slot, part, CORE + SIZE :, :] = zero

    for load in loads[2:]:
        load.wait()

    for step in range(ITERS):
        halo_second(step, 0, first0)
        halo_second(step, 1, first1)
        halo_last(step, 0, first0)
        forward_first(ext, offs, probe, prop, tables, psi)
        halo_last(step, 1, first1)
        middle(ext, offs, counts, measured, tables, psi, back, padded.at[1])
        sums1 = reduce_first(step, 1)
        backward_first(offs, probe, prop, tables, back, padded.at[0])
        reduce_second(step, 1, sums1)
        sums0 = reduce_first(step, 0)
        reduce_second(step, 0, sums0)
        for s, sums in ((0, sums0), (1, sums1)):
            new = reduce_last(step, s, sums)
            if step < ITERS - 1:
                own[step + 1, s] = new
                copies = halo_first(step + 1, s)
                if s == 0:
                    first0 = copies
                else:
                    first1 = copies
            else:
                out[0, s] = new[:, :CORE]
                out[1, s] = pltpu.roll(new, CORE, 1)[:, :CORE]
    for copy in started:
        copy.wait_send()


def solution(mesh):
    shape = (mesh.shape["ty"], mesh.shape["tx"])
    vmem = pl.BlockSpec(memory_space=pltpu.VMEM)
    hbm = pl.BlockSpec(memory_space=pl.ANY)
    tables = dft_blocks()

    def on_device(
        transmission, probe_field, propagator_phase, scan_offsets, position_counts, intensities
    ):
        tile = (CORE, SIZE)
        field = (SIZE, SIZE)
        return pl.pallas_call(
            functools.partial(kernel, shape),
            out_shape=jax.ShapeDtypeStruct(transmission.shape, F32),
            in_specs=[hbm] * 7,
            out_specs=vmem,
            scratch_shapes=[
                pltpu.VMEM(transmission.shape, F32),
                pltpu.VMEM((2,) + field, F32),
                pltpu.VMEM(field, F32),
                pltpu.SMEM((1, 1, 2, SLOTS), jnp.int32),
                pltpu.SMEM((1, 1), jnp.int32),
                pltpu.VMEM(intensities.shape, F32),
                pltpu.VMEM(tables.shape, BF16),
                pltpu.VMEM((ITERS, 2) + tile, F32),
                pltpu.VMEM((ITERS, 2, 8) + tile, F32),
                pltpu.VMEM((ITERS, 2, 3, 3) + tile, F32),
                pltpu.VMEM((ITERS, 2, 3) + tile, F32),
                pltpu.VMEM((ITERS, 2, 5) + tile, F32),
                pltpu.VMEM((2, 3, 3 * CORE, SIZE), F32),
                pltpu.VMEM((2,) + field, F32),
                pltpu.VMEM((SLOTS, 2) + field, F32),
                pltpu.VMEM((SLOTS, 2) + field, F32),
                pltpu.VMEM((2, SLOTS, 2, 2 * SIZE, SIZE), F32),
                pltpu.SemaphoreType.DMA((ITERS, 2, COPIES)),
                pltpu.SemaphoreType.DMA((ITERS, 2, COPIES)),
                pltpu.SemaphoreType.DMA((7,)),
            ],
            compiler_params=pltpu.CompilerParams(
                collective_id=0, has_side_effects=True, vmem_limit_bytes=60 * 1024 * 1024
            ),
        )(
            transmission,
            probe_field,
            propagator_phase,
            jnp.swapaxes(scan_offsets, 2, 3),
            position_counts,
            intensities,
            jnp.asarray(tables),
        )

    return jax.shard_map(
        on_device,
        mesh=mesh,
        in_specs=(
            P(None, None, "ty", "tx"),
            P(),
            P(),
            P("ty", "tx", None, None),
            P("ty", "tx"),
            P("ty", "tx", None, None, None),
        ),
        out_specs=P(None, None, "ty", "tx"),
        check_vma=False,
    )
```

```python
import functools
import math

import jax
import jax.numpy as jnp
import numpy as np
from jax import lax
from jax.experimental import pallas as pl
from jax.experimental.pallas import tpu as pltpu
from jax.sharding import PartitionSpec as P

ITERS = 2
STEP = 0.003
SIZE = 128
CORE = 64
SLOTS = 6
F32 = jnp.float32
BF16 = jnp.bfloat16

UP, DOWN, OUT, PAIR, OUT_UP, OUT_DOWN, PAIR_UP, PAIR_DOWN = range(8)
ROW_UP, ROW_DOWN, ROW_OWN = range(3)
ROW_START = (0, 128, 64)
COL_OUT, COL_OWN, COL_PAIR = range(3)
ADD_PAIR, CORNER_UP, CORNER_DOWN, ADD_UP, ADD_DOWN, ADD_OUT = range(6)
COPIES = 14


def dft_blocks():
    index = np.arange(SIZE)
    angle = 2.0 * math.pi / SIZE * ((index[:, None] * index[None, :]) % SIZE)
    re = np.cos(angle) / math.sqrt(SIZE)
    im = -np.sin(angle) / math.sqrt(SIZE)
    right = np.block([[re, im], [-im, re]])
    blocks = np.stack([right, right.T])
    high = blocks.astype(BF16)
    low = (blocks - high.astype(np.float64)).astype(BF16)
    return np.stack([high, low], axis=1)


def split(x):
    high = x.astype(BF16)
    return high, (x - high.astype(F32)).astype(BF16)


def dot(a, b):
    return jnp.dot(a, b, preferred_element_type=F32)


def from_right(fields, table):
    high, low = split(
        jnp.concatenate(
            [
                jnp.concatenate([fields[0], fields[1]], axis=1),
                jnp.concatenate([fields[2], fields[3]], axis=1),
            ],
            axis=0,
        )
    )
    out = dot(high, table[0]) + dot(low, table[0]) + dot(high, table[1])
    return out[:SIZE, :SIZE], out[:SIZE, SIZE:], out[SIZE:, :SIZE], out[SIZE:, SIZE:]


def from_left(fields, table):
    high, low = split(
        jnp.concatenate(
            [
                jnp.concatenate([fields[0], fields[2]], axis=1),
                jnp.concatenate([fields[1], fields[3]], axis=1),
            ],
            axis=0,
        )
    )
    out = dot(table[0], high) + dot(table[0], low) + dot(table[1], high)
    return out[:SIZE, :SIZE], out[SIZE:, :SIZE], out[:SIZE, SIZE:], out[SIZE:, SIZE:]


def times(a, b):
    return a[0] * b[0] - a[1] * b[1], a[0] * b[1] + a[1] * b[0]


def times_conj(a, b):
    return a[0] * b[0] + a[1] * b[1], a[1] * b[0] - a[0] * b[1]


def lanes_of(shape):
    return lax.broadcasted_iota(jnp.int32, shape, 1)


def load_window(ext, offs, slice_, slot):
    row, col = offs[0, 0, 0, slot], offs[0, 0, 1, slot]
    rows = pl.ds(row, SIZE)
    back = lax.rem(SIZE - col, SIZE)
    keep = lanes_of((SIZE, SIZE)) < SIZE - col
    last = ext[slice_, 2, rows, :]
    re = jnp.where(
        keep, pltpu.roll(ext[slice_, 0, rows, :], back, 1), pltpu.roll(last, back, 1)
    )
    im = jnp.where(
        keep, pltpu.roll(ext[slice_, 1, rows, :], back, 1), pltpu.roll(last, CORE - col, 1)
    )
    return re, im


def store_field(padded, offs, slot, field):
    col = offs[0, 0, 1, slot]
    for part in range(2):
        padded[slot, part, CORE : CORE + SIZE, :] = pltpu.roll(field[part], col, 1)


def gradient_rows(padded, offs, start):
    lane = lanes_of((CORE, SIZE))
    sums = [jnp.zeros((CORE, SIZE), F32) for _ in range(4)]
    for slot in range(SLOTS):
        row, col = offs[0, 0, 0, slot], offs[0, 0, 1, slot]
        rows = pl.ds(CORE + start - row, CORE)
        here = lane >= col
        for part in range(2):
            value = padded[slot, part, rows, :]
            sums[part] = sums[part] + jnp.where(here, value, 0.0)
            sums[2 + part] = sums[2 + part] + jnp.where(here, 0.0, value)
    low = lane < CORE
    first = jnp.where(low, sums[0], pltpu.roll(sums[1], CORE, 1))
    second = jnp.where(low, pltpu.roll(sums[0], CORE, 1), sums[1])
    third = jnp.where(low, sums[2], pltpu.roll(sums[3], CORE, 1))
    return first, second, third


def transform(fields, tables, which, left_first=False):
    order = (from_left, from_right) if left_first else (from_right, from_left)
    for apply in order:
        fields = [apply(field, tables[which[0]] if apply is from_right else tables[which[1]]) for field in fields]
    return fields


FORWARD, INVERSE = (0, 1), (1, 0)
PAIRS = tuple((2 * pair, 2 * pair + 1) for pair in range(SLOTS // 2))


def forward_first(ext, offs, probe, prop, tables, psi):
    light = (probe[0], probe[1])
    fields = [
        times(light, load_window(ext, offs, 0, a)) + times(light, load_window(ext, offs, 0, b))
        for a, b in PAIRS
    ]
    fields = transform(fields, tables, FORWARD)
    factor = (prop[0], prop[1])
    fields = [times(field[:2], factor) + times(field[2:], factor) for field in fields]
    fields = transform(fields, tables, INVERSE, True)
    for slots, field in zip(PAIRS, fields):
        for n, slot in enumerate(slots):
            for part in range(2):
                psi[slot, part] = field[2 * n + part]


def middle(ext, offs, counts, measured, tables, psi, back, wins, padded):
    fields = []
    for slots in PAIRS:
        field = ()
        for slot in slots:
            window = load_window(ext, offs, 1, slot)
            wins[slot, 0] = window[0]
            wins[slot, 1] = window[1]
            field += times((psi[slot, 0], psi[slot, 1]), window)
        fields.append(field)
    fields = transform(fields, tables, FORWARD)
    grads = []
    for slots, field in zip(PAIRS, fields):
        grad = ()
        for n, slot in enumerate(slots):
            re, im = field[2 * n], field[2 * n + 1]
            live = jnp.where(slot < counts[0, 0], 4.0, 0.0)
            factor = live * (re * re + im * im - measured[0, 0, slot])
            grad += (factor * re, factor * im)
        grads.append(grad)
    grads = transform(grads, tables, INVERSE, True)
    for slots, both in zip(PAIRS, grads):
        for n, slot in enumerate(slots):
            grad = both[2 * n : 2 * n + 2]
            field = times_conj(grad, (wins[slot, 0], wins[slot, 1]))
            for part in range(2):
                back[slot, part] = field[part]
            store_field(
                padded, offs, slot, times_conj(grad, (psi[slot, 0], psi[slot, 1]))
            )


def backward_first(offs, probe, prop, tables, back, padded):
    fields = [
        (back[a, 0], back[a, 1], back[b, 0], back[b, 1]) for a, b in PAIRS
    ]
    fields = transform(fields, tables, FORWARD)
    factor = (prop[0], prop[1])
    fields = [times_conj(field[:2], factor) + times_conj(field[2:], factor) for field in fields]
    fields = transform(fields, tables, INVERSE, True)
    light = (probe[0], probe[1])
    for slots, field in zip(PAIRS, fields):
        for n, slot in enumerate(slots):
            store_field(
                padded, offs, slot, times_conj(field[2 * n : 2 * n + 2], light)
            )


def kernel(
    mesh_shape,
    obj_in,
    probe_in,
    phase_in,
    offs_in,
    counts_in,
    measured_in,
    tables_in,
    out,
    obj,
    probe,
    phase,
    offs,
    counts,
    measured,
    tables,
    own,
    halo,
    grads,
    passed,
    added,
    ext,
    prop,
    psi,
    back,
    wins,
    padded,
    send_sems,
    recv_sems,
    load_sems,
):
    ty_count, tx_count = mesh_shape
    row, col = lax.axis_index("ty"), lax.axis_index("tx")
    even = lax.rem(col, 2) == 0
    up = lax.rem(row + ty_count - 1, ty_count)
    down = lax.rem(row + 1, ty_count)
    right = lax.rem(col + 1, tx_count)
    left = lax.rem(col + tx_count - 1, tx_count)
    side = jnp.where(even, left, right)
    outer = {"ty": row, "tx": side}
    partner = {"ty": row, "tx": jnp.where(even, right, left)}
    above, below = {"ty": up, "tx": col}, {"ty": down, "tx": col}
    outer_above, outer_below = {"ty": up, "tx": side}, {"ty": down, "tx": side}
    has_above = row > 0
    has_below = row < ty_count - 1
    has_outer = jnp.logical_and(col > 0, col < tx_count - 1)

    barrier = pltpu.get_barrier_semaphore()
    for target in (outer, outer_above, outer_below, above, below, partner):
        pl.semaphore_signal(
            barrier, inc=1, device_id=target, device_id_type=pl.DeviceIdType.MESH
        )

    loads = [
        pltpu.make_async_copy(src, dst, load_sems.at[n])
        for n, (src, dst) in enumerate(
            (
                (obj_in, obj),
                (phase_in, phase),
                (offs_in, offs),
                (counts_in, counts),
                (probe_in, probe),
                (tables_in, tables),
                (measured_in, measured),
            )
        )
    ]
    for load in loads:
        load.start()

    low = lanes_of((CORE, SIZE)) < CORE
    loads[0].wait()
    for s in range(2):
        own[0, s] = jnp.concatenate([obj[0, s], obj[1, s]], axis=1)
    pl.semaphore_wait(barrier, 6)

    started = []

    def send(src, dst, step, s, kind, target):
        copy = pltpu.make_async_remote_copy(
            src_ref=src,
            dst_ref=dst,
            send_sem=send_sems.at[step, s, kind],
            recv_sem=recv_sems.at[step, s, kind],
            device_id=target,
            device_id_type=pl.DeviceIdType.MESH,
        )
        copy.start()
        started.append(copy)
        return copy

    def send_halo(step, s, kind, src, target):
        return send(src, halo.at[step, s, kind], step, s, kind, target)

    def halo_first(step, s):
        mine = own.at[step, s]
        return {
            kind: send_halo(step, s, kind, mine, target)
            for kind, target in (
                (OUT, outer),
                (OUT_DOWN, outer_above),
                (OUT_UP, outer_below),
                (DOWN, above),
                (UP, below),
                (PAIR, partner),
            )
        }

    def halo_second(step, s, copies):
        for kind, passed_on in ((UP, PAIR_UP), (DOWN, PAIR_DOWN)):
            copies[kind].wait_recv()
            copies[passed_on] = send_halo(
                step, s, passed_on, halo.at[step, s, kind], partner
            )

    def place(s, start, out_tile, own_tile, pair_tile):
        first = jnp.where(even, out_tile, pair_tile)
        third = jnp.where(even, pair_tile, out_tile)
        rows = slice(start, start + CORE)
        ext[s, 0, rows, :] = jnp.where(low, first, pltpu.roll(own_tile, CORE, 1))
        ext[s, 1, rows, :] = jnp.where(low, pltpu.roll(first, CORE, 1), own_tile)
        ext[s, 2, rows, :] = third

    def halo_last(step, s, copies):
        for kind in (PAIR, PAIR_UP, PAIR_DOWN, OUT_UP, OUT_DOWN, OUT):
            copies[kind].wait_recv()
        tile = lambda kind, ok: jnp.where(ok, halo[step, s, kind], 0.0)
        both = jnp.logical_and
        place(s, CORE, tile(OUT, has_outer), own[step, s], halo[step, s, PAIR])
        place(
            s,
            0,
            tile(OUT_UP, both(has_outer, has_above)),
            tile(UP, has_above),
            tile(PAIR_UP, has_above),
        )
        place(
            s,
            2 * CORE,
            tile(OUT_DOWN, both(has_outer, has_below)),
            tile(DOWN, has_below),
            tile(PAIR_DOWN, has_below),
        )

    def reduce_first(step, s):
        sent = grads.at[step, s]
        copies = {}
        for tile, kind, target in (
            (ROW_UP, CORNER_DOWN, outer_above),
            (ROW_DOWN, CORNER_UP, outer_below),
            (ROW_OWN, ADD_OUT, outer),
        ):
            first, second, third = gradient_rows(padded.at[s], offs, ROW_START[tile])
            sent[COL_OUT, tile] = jnp.where(even, first, third)
            copies[kind] = send(
                sent.at[COL_OUT, tile],
                added.at[step, s, kind - 1],
                step,
                s,
                8 + kind,
                target,
            )
            sent[COL_PAIR, tile] = jnp.where(even, third, first)
            sent[COL_OWN, tile] = second
        copies[ADD_PAIR] = send(
            sent.at[COL_PAIR], passed.at[step, s], step, s, 8 + ADD_PAIR, partner
        )
        return copies

    def masked(step, s, kind, ok):
        return jnp.where(ok, added[step, s, kind - 1], 0.0)

    def reduce_second(step, s, copies):
        mine = grads.at[step, s]
        copies[ADD_PAIR].wait_recv()
        for tile, kind, target in ((ROW_UP, ADD_DOWN, above), (ROW_DOWN, ADD_UP, below)):
            mine[COL_OWN, tile] = mine[COL_OWN, tile] + passed[step, s, tile]
            copies[kind] = send(
                mine.at[COL_OWN, tile],
                added.at[step, s, kind - 1],
                step,
                s,
                8 + kind,
                target,
            )

    def reduce_last(step, s, copies):
        total = grads[step, s, COL_OWN, ROW_OWN] + passed[step, s, ROW_OWN]
        both = jnp.logical_and
        for kind, ok in (
            (ADD_UP, has_above),
            (ADD_DOWN, has_below),
            (CORNER_UP, both(has_above, has_outer)),
            (CORNER_DOWN, both(has_below, has_outer)),
            (ADD_OUT, has_outer),
        ):
            copies[kind].wait_recv()
            total = total + masked(step, s, kind, ok)
        return own[step, s] - STEP * total

    first0 = halo_first(0, 0)
    first1 = halo_first(0, 1)
    loads[1].wait()
    prop[0] = jnp.cos(phase[...])
    prop[1] = jnp.sin(phase[...])
    zero = jnp.zeros((CORE, SIZE), F32)
    for s in range(2):
        for slot in range(SLOTS):
            for part in range(2):
                padded[s, slot, part, :CORE, :] = zero
                padded[s, slot, part, CORE + SIZE :, :] = zero

    for load in loads[2:]:
        load.wait()

    for step in range(ITERS):
        halo_second(step, 0, first0)
        halo_second(step, 1, first1)
        halo_last(step, 0, first0)
        forward_first(ext, offs, probe, prop, tables, psi)
        halo_last(step, 1, first1)
        middle(ext, offs, counts, measured, tables, psi, back, wins, padded.at[1])
        sums1 = reduce_first(step, 1)
        backward_first(offs, probe, prop, tables, back, padded.at[0])
        reduce_second(step, 1, sums1)
        sums0 = reduce_first(step, 0)
        reduce_second(step, 0, sums0)
        for s, sums in ((0, sums0), (1, sums1)):
            new = reduce_last(step, s, sums)
            if step < ITERS - 1:
                own[step + 1, s] = new
                copies = halo_first(step + 1, s)
                if s == 0:
                    first0 = copies
                else:
                    first1 = copies
            else:
                out[0, s] = new[:, :CORE]
                out[1, s] = pltpu.roll(new, CORE, 1)[:, :CORE]
    for copy in started:
        copy.wait_send()


def solution(mesh):
    shape = (mesh.shape["ty"], mesh.shape["tx"])
    vmem = pl.BlockSpec(memory_space=pltpu.VMEM)
    hbm = pl.BlockSpec(memory_space=pl.ANY)
    tables = dft_blocks()

    def on_device(
        transmission, probe_field, propagator_phase, scan_offsets, position_counts, intensities
    ):
        tile = (CORE, SIZE)
        field = (SIZE, SIZE)
        return pl.pallas_call(
            functools.partial(kernel, shape),
            out_shape=jax.ShapeDtypeStruct(transmission.shape, F32),
            in_specs=[hbm] * 7,
            out_specs=vmem,
            scratch_shapes=[
                pltpu.VMEM(transmission.shape, F32),
                pltpu.VMEM((2,) + field, F32),
                pltpu.VMEM(field, F32),
                pltpu.SMEM((1, 1, 2, SLOTS), jnp.int32),
                pltpu.SMEM((1, 1), jnp.int32),
                pltpu.VMEM(intensities.shape, F32),
                pltpu.VMEM(tables.shape, BF16),
                pltpu.VMEM((ITERS, 2) + tile, F32),
                pltpu.VMEM((ITERS, 2, 8) + tile, F32),
                pltpu.VMEM((ITERS, 2, 3, 3) + tile, F32),
                pltpu.VMEM((ITERS, 2, 3) + tile, F32),
                pltpu.VMEM((ITERS, 2, 5) + tile, F32),
                pltpu.VMEM((2, 3, 3 * CORE, SIZE), F32),
                pltpu.VMEM((2,) + field, F32),
                pltpu.VMEM((SLOTS, 2) + field, F32),
                pltpu.VMEM((SLOTS, 2) + field, F32),
                pltpu.VMEM((SLOTS, 2) + field, F32),
                pltpu.VMEM((2, SLOTS, 2, 2 * SIZE, SIZE), F32),
                pltpu.SemaphoreType.DMA((ITERS, 2, COPIES)),
                pltpu.SemaphoreType.DMA((ITERS, 2, COPIES)),
                pltpu.SemaphoreType.DMA((7,)),
            ],
            compiler_params=pltpu.CompilerParams(
                collective_id=0, has_side_effects=True, vmem_limit_bytes=60 * 1024 * 1024
            ),
        )(
            transmission,
            probe_field,
            propagator_phase,
            jnp.swapaxes(scan_offsets, 2, 3),
            position_counts,
            intensities,
            jnp.asarray(tables),
        )

    return jax.shard_map(
        on_device,
        mesh=mesh,
        in_specs=(
            P(None, None, "ty", "tx"),
            P(),
            P(),
            P("ty", "tx", None, None),
            P("ty", "tx"),
            P("ty", "tx", None, None, None),
        ),
        out_specs=P(None, None, "ty", "tx"),
        check_vma=False,
    )
```

```python
import functools
import math

import jax
import jax.numpy as jnp
import numpy as np
from jax import lax
from jax.experimental import pallas as pl
from jax.experimental.pallas import tpu as pltpu
from jax.sharding import PartitionSpec as P

ITERS = 2
STEP = 0.003
SIZE = 128
CORE = 64
SLOTS = 6
F32 = jnp.float32
BF16 = jnp.bfloat16

UP, DOWN, OUT, PAIR, OUT_UP, OUT_DOWN, PAIR_UP, PAIR_DOWN = range(8)
ROW_UP, ROW_DOWN, ROW_OWN = range(3)
ROW_START = (0, 128, 64)
COL_OUT, COL_OWN, COL_PAIR = range(3)
ADD_PAIR, CORNER_UP, CORNER_DOWN, ADD_UP, ADD_DOWN, ADD_OUT = range(6)
COPIES = 14


def dft_blocks():
    index = np.arange(SIZE)
    angle = 2.0 * math.pi / SIZE * ((index[:, None] * index[None, :]) % SIZE)
    re = np.cos(angle) / math.sqrt(SIZE)
    im = -np.sin(angle) / math.sqrt(SIZE)
    right = np.block([[re, im], [-im, re]])
    blocks = np.stack([right, right.T])
    high = blocks.astype(BF16)
    low = (blocks - high.astype(np.float64)).astype(BF16)
    return np.stack([high, low], axis=1)


def split(x):
    high = x.astype(BF16)
    return high, (x - high.astype(F32)).astype(BF16)


def dot(a, b):
    return jnp.dot(a, b, preferred_element_type=F32)


def from_right(fields, table):
    high, low = split(
        jnp.concatenate(
            [
                jnp.concatenate([fields[0], fields[1]], axis=1),
                jnp.concatenate([fields[2], fields[3]], axis=1),
            ],
            axis=0,
        )
    )
    out = dot(high, table[0]) + dot(low, table[0]) + dot(high, table[1])
    return out[:SIZE, :SIZE], out[:SIZE, SIZE:], out[SIZE:, :SIZE], out[SIZE:, SIZE:]


def from_left(fields, table):
    high, low = split(
        jnp.concatenate(
            [
                jnp.concatenate([fields[0], fields[2]], axis=1),
                jnp.concatenate([fields[1], fields[3]], axis=1),
            ],
            axis=0,
        )
    )
    out = dot(table[0], high) + dot(table[0], low) + dot(table[1], high)
    return out[:SIZE, :SIZE], out[SIZE:, :SIZE], out[:SIZE, SIZE:], out[SIZE:, SIZE:]


def times(a, b):
    return a[0] * b[0] - a[1] * b[1], a[0] * b[1] + a[1] * b[0]


def times_conj(a, b):
    return a[0] * b[0] + a[1] * b[1], a[1] * b[0] - a[0] * b[1]


def lanes_of(shape):
    return lax.broadcasted_iota(jnp.int32, shape, 1)


def load_window(ext, offs, slice_, slot):
    row, col = offs[0, 0, 0, slot], offs[0, 0, 1, slot]
    rows = pl.ds(row, SIZE)
    back = lax.rem(SIZE - col, SIZE)
    keep = lanes_of((SIZE, SIZE)) < SIZE - col
    last = ext[slice_, 2, rows, :]
    re = jnp.where(
        keep, pltpu.roll(ext[slice_, 0, rows, :], back, 1), pltpu.roll(last, back, 1)
    )
    im = jnp.where(
        keep, pltpu.roll(ext[slice_, 1, rows, :], back, 1), pltpu.roll(last, CORE - col, 1)
    )
    return re, im


def store_field(padded, offs, slot, field):
    col = offs[0, 0, 1, slot]
    for part in range(2):
        padded[slot, part, CORE : CORE + SIZE, :] = pltpu.roll(field[part], col, 1)


def gradient_rows(padded, offs, start):
    lane = lanes_of((CORE, SIZE))
    sums = [jnp.zeros((CORE, SIZE), F32) for _ in range(4)]
    for slot in range(SLOTS):
        row, col = offs[0, 0, 0, slot], offs[0, 0, 1, slot]
        rows = pl.ds(CORE + start - row, CORE)
        here = lane >= col
        for part in range(2):
            value = padded[slot, part, rows, :]
            sums[part] = sums[part] + jnp.where(here, value, 0.0)
            sums[2 + part] = sums[2 + part] + jnp.where(here, 0.0, value)
    low = lane < CORE
    first = jnp.where(low, sums[0], pltpu.roll(sums[1], CORE, 1))
    second = jnp.where(low, pltpu.roll(sums[0], CORE, 1), sums[1])
    third = jnp.where(low, sums[2], pltpu.roll(sums[3], CORE, 1))
    return first, second, third


def transform(fields, tables, which, left_first=False):
    order = (from_left, from_right) if left_first else (from_right, from_left)
    for apply in order:
        fields = [apply(field, tables[which[0]] if apply is from_right else tables[which[1]]) for field in fields]
    return fields


FORWARD, INVERSE = (0, 1), (1, 0)
PAIRS = tuple((2 * pair, 2 * pair + 1) for pair in range(SLOTS // 2))


def forward_first(ext, offs, probe, prop, tables, psi, between):
    light = (probe[0], probe[1])
    fields = [
        times(light, load_window(ext, offs, 0, a)) + times(light, load_window(ext, offs, 0, b))
        for a, b in PAIRS
    ]
    fields = transform(fields, tables, FORWARD)
    factor = (prop[0], prop[1])
    fields = [times(field[:2], factor) + times(field[2:], factor) for field in fields]
    between()
    fields = transform(fields, tables, INVERSE, True)
    for slots, field in zip(PAIRS, fields):
        for n, slot in enumerate(slots):
            for part in range(2):
                psi[slot, part] = field[2 * n + part]


def middle(ext, offs, counts, measured, tables, psi, back, wins, padded):
    fields = []
    for slots in PAIRS:
        field = ()
        for slot in slots:
            window = load_window(ext, offs, 1, slot)
            wins[slot, 0] = window[0]
            wins[slot, 1] = window[1]
            field += times((psi[slot, 0], psi[slot, 1]), window)
        fields.append(field)
    fields = transform(fields, tables, FORWARD)
    grads = []
    for slots, field in zip(PAIRS, fields):
        grad = ()
        for n, slot in enumerate(slots):
            re, im = field[2 * n], field[2 * n + 1]
            live = jnp.where(slot < counts[0, 0], 4.0, 0.0)
            factor = live * (re * re + im * im - measured[0, 0, slot])
            grad += (factor * re, factor * im)
        grads.append(grad)
    grads = transform(grads, tables, INVERSE, True)
    for slots, both in zip(PAIRS, grads):
        for n, slot in enumerate(slots):
            grad = both[2 * n : 2 * n + 2]
            field = times_conj(grad, (wins[slot, 0], wins[slot, 1]))
            for part in range(2):
                back[slot, part] = field[part]
            store_field(
                padded, offs, slot, times_conj(grad, (psi[slot, 0], psi[slot, 1]))
            )


def backward_first(offs, probe, prop, tables, back, padded, between):
    fields = [
        (back[a, 0], back[a, 1], back[b, 0], back[b, 1]) for a, b in PAIRS
    ]
    fields = transform(fields, tables, FORWARD)
    factor = (prop[0], prop[1])
    fields = [times_conj(field[:2], factor) + times_conj(field[2:], factor) for field in fields]
    between()
    fields = transform(fields, tables, INVERSE, True)
    light = (probe[0], probe[1])
    for slots, field in zip(PAIRS, fields):
        for n, slot in enumerate(slots):
            store_field(
                padded, offs, slot, times_conj(field[2 * n : 2 * n + 2], light)
            )


def kernel(
    mesh_shape,
    obj_in,
    probe_in,
    phase_in,
    offs_in,
    counts_in,
    measured_in,
    tables_in,
    out,
    obj,
    probe,
    phase,
    offs,
    counts,
    measured,
    tables,
    own,
    halo,
    grads,
    passed,
    added,
    ext,
    prop,
    psi,
    back,
    wins,
    padded,
    send_sems,
    recv_sems,
    load_sems,
):
    ty_count, tx_count = mesh_shape
    row, col = lax.axis_index("ty"), lax.axis_index("tx")
    even = lax.rem(col, 2) == 0
    up = lax.rem(row + ty_count - 1, ty_count)
    down = lax.rem(row + 1, ty_count)
    right = lax.rem(col + 1, tx_count)
    left = lax.rem(col + tx_count - 1, tx_count)
    side = jnp.where(even, left, right)
    outer = {"ty": row, "tx": side}
    partner = {"ty": row, "tx": jnp.where(even, right, left)}
    above, below = {"ty": up, "tx": col}, {"ty": down, "tx": col}
    outer_above, outer_below = {"ty": up, "tx": side}, {"ty": down, "tx": side}
    has_above = row > 0
    has_below = row < ty_count - 1
    has_outer = jnp.logical_and(col > 0, col < tx_count - 1)

    barrier = pltpu.get_barrier_semaphore()
    for target in (outer, outer_above, outer_below, above, below, partner):
        pl.semaphore_signal(
            barrier, inc=1, device_id=target, device_id_type=pl.DeviceIdType.MESH
        )

    loads = [
        pltpu.make_async_copy(src, dst, load_sems.at[n])
        for n, (src, dst) in enumerate(
            (
                (obj_in, obj),
                (phase_in, phase),
                (offs_in, offs),
                (counts_in, counts),
                (probe_in, probe),
                (tables_in, tables),
                (measured_in, measured),
            )
        )
    ]
    for load in loads:
        load.start()

    low = lanes_of((CORE, SIZE)) < CORE
    loads[0].wait()
    for s in range(2):
        own[0, s] = jnp.concatenate([obj[0, s], obj[1, s]], axis=1)
    pl.semaphore_wait(barrier, 6)

    started = []

    def send(src, dst, step, s, kind, target):
        copy = pltpu.make_async_remote_copy(
            src_ref=src,
            dst_ref=dst,
            send_sem=send_sems.at[step, s, kind],
            recv_sem=recv_sems.at[step, s, kind],
            device_id=target,
            device_id_type=pl.DeviceIdType.MESH,
        )
        copy.start()
        started.append(copy)
        return copy

    def send_halo(step, s, kind, src, target):
        return send(src, halo.at[step, s, kind], step, s, kind, target)

    def halo_first(step, s):
        mine = own.at[step, s]
        return {
            kind: send_halo(step, s, kind, mine, target)
            for kind, target in (
                (OUT, outer),
                (OUT_DOWN, outer_above),
                (OUT_UP, outer_below),
                (DOWN, above),
                (UP, below),
                (PAIR, partner),
            )
        }

    def halo_second(step, s, copies):
        for kind, passed_on in ((UP, PAIR_UP), (DOWN, PAIR_DOWN)):
            copies[kind].wait_recv()
            copies[passed_on] = send_halo(
                step, s, passed_on, halo.at[step, s, kind], partner
            )

    def place(s, start, out_tile, own_tile, pair_tile):
        first = jnp.where(even, out_tile, pair_tile)
        third = jnp.where(even, pair_tile, out_tile)
        rows = slice(start, start + CORE)
        ext[s, 0, rows, :] = jnp.where(low, first, pltpu.roll(own_tile, CORE, 1))
        ext[s, 1, rows, :] = jnp.where(low, pltpu.roll(first, CORE, 1), own_tile)
        ext[s, 2, rows, :] = third

    def halo_last(step, s, copies):
        for kind in (PAIR, PAIR_UP, PAIR_DOWN, OUT_UP, OUT_DOWN, OUT):
            copies[kind].wait_recv()
        tile = lambda kind, ok: jnp.where(ok, halo[step, s, kind], 0.0)
        both = jnp.logical_and
        place(s, CORE, tile(OUT, has_outer), own[step, s], halo[step, s, PAIR])
        place(
            s,
            0,
            tile(OUT_UP, both(has_outer, has_above)),
            tile(UP, has_above),
            tile(PAIR_UP, has_above),
        )
        place(
            s,
            2 * CORE,
            tile(OUT_DOWN, both(has_outer, has_below)),
            tile(DOWN, has_below),
            tile(PAIR_DOWN, has_below),
        )

    def reduce_rows(step, s, send_now):
        sent = grads.at[step, s]
        for tile in (ROW_UP, ROW_DOWN, ROW_OWN):
            first, second, third = gradient_rows(padded.at[s], offs, ROW_START[tile])
            sent[COL_OUT, tile] = jnp.where(even, first, third)
            sent[COL_PAIR, tile] = jnp.where(even, third, first)
            sent[COL_OWN, tile] = second
            send_now(tile)

    def send_sum(step, s, kind, src, target):
        return send(src, added.at[step, s, kind - 1], step, s, 8 + kind, target)

    def reduce_first(step, s, copies, tile):
        kind, target = {
            ROW_UP: (CORNER_DOWN, outer_above),
            ROW_DOWN: (CORNER_UP, outer_below),
            ROW_OWN: (ADD_OUT, outer),
        }[tile]
        copies[kind] = send_sum(step, s, kind, grads.at[step, s, COL_OUT, tile], target)
        if tile == ROW_OWN:
            copies[ADD_PAIR] = send(
                grads.at[step, s, COL_PAIR],
                passed.at[step, s],
                step,
                s,
                8 + ADD_PAIR,
                partner,
            )

    def masked(step, s, kind, ok):
        return jnp.where(ok, added[step, s, kind - 1], 0.0)

    def reduce_second(step, s, copies):
        mine = grads.at[step, s]
        copies[ADD_PAIR].wait_recv()
        for tile, kind, target in ((ROW_UP, ADD_DOWN, above), (ROW_DOWN, ADD_UP, below)):
            mine[COL_OWN, tile] = mine[COL_OWN, tile] + passed[step, s, tile]
            copies[kind] = send_sum(step, s, kind, mine.at[COL_OWN, tile], target)

    def reduce_last(step, s, copies):
        total = grads[step, s, COL_OWN, ROW_OWN] + passed[step, s, ROW_OWN]
        both = jnp.logical_and
        for kind, ok in (
            (ADD_UP, has_above),
            (ADD_DOWN, has_below),
            (CORNER_UP, both(has_above, has_outer)),
            (CORNER_DOWN, both(has_below, has_outer)),
            (ADD_OUT, has_outer),
        ):
            copies[kind].wait_recv()
            total = total + masked(step, s, kind, ok)
        return own[step, s] - STEP * total

    first0 = halo_first(0, 0)
    first1 = halo_first(0, 1)
    loads[1].wait()
    prop[0] = jnp.cos(phase[...])
    prop[1] = jnp.sin(phase[...])
    zero = jnp.zeros((CORE, SIZE), F32)
    for s in range(2):
        for slot in range(SLOTS):
            for part in range(2):
                padded[s, slot, part, :CORE, :] = zero
                padded[s, slot, part, CORE + SIZE :, :] = zero

    for load in loads[2:]:
        load.wait()

    for step in range(ITERS):
        halo_second(step, 0, first0)
        halo_last(step, 0, first0)
        pass_halo = functools.partial(halo_second, step, 1, first1)
        forward_first(ext, offs, probe, prop, tables, psi, pass_halo)
        halo_last(step, 1, first1)
        middle(ext, offs, counts, measured, tables, psi, back, wins, padded.at[1])
        sums0, sums1 = {}, {}
        first_sums = functools.partial(reduce_first, step, 0, sums0)
        last = step == ITERS - 1
        if last:
            reduce_rows(step, 1, functools.partial(reduce_first, step, 1, sums1))

        def pass_sums():
            if last:
                reduce_second(step, 1, sums1)

        backward_first(offs, probe, prop, tables, back, padded.at[0], pass_sums)
        reduce_rows(step, 0, first_sums)
        if not last:
            reduce_rows(step, 1, lambda tile: None)
        reduce_second(step, 0, sums0)
        if not last:
            for tile in (ROW_UP, ROW_DOWN, ROW_OWN):
                reduce_first(step, 1, sums1, tile)
            reduce_second(step, 1, sums1)
        for s, sums in ((0, sums0), (1, sums1)):
            new = reduce_last(step, s, sums)
            if step < ITERS - 1:
                own[step + 1, s] = new
                copies = halo_first(step + 1, s)
                if s == 0:
                    first0 = copies
                else:
                    first1 = copies
            else:
                out[0, s] = new[:, :CORE]
                out[1, s] = pltpu.roll(new, CORE, 1)[:, :CORE]
    for copy in started:
        copy.wait_send()


def solution(mesh):
    shape = (mesh.shape["ty"], mesh.shape["tx"])
    vmem = pl.BlockSpec(memory_space=pltpu.VMEM)
    hbm = pl.BlockSpec(memory_space=pl.ANY)
    tables = dft_blocks()

    def on_device(
        transmission, probe_field, propagator_phase, scan_offsets, position_counts, intensities
    ):
        tile = (CORE, SIZE)
        field = (SIZE, SIZE)
        return pl.pallas_call(
            functools.partial(kernel, shape),
            out_shape=jax.ShapeDtypeStruct(transmission.shape, F32),
            in_specs=[hbm] * 7,
            out_specs=vmem,
            scratch_shapes=[
                pltpu.VMEM(transmission.shape, F32),
                pltpu.VMEM((2,) + field, F32),
                pltpu.VMEM(field, F32),
                pltpu.SMEM((1, 1, 2, SLOTS), jnp.int32),
                pltpu.SMEM((1, 1), jnp.int32),
                pltpu.VMEM(intensities.shape, F32),
                pltpu.VMEM(tables.shape, BF16),
                pltpu.VMEM((ITERS, 2) + tile, F32),
                pltpu.VMEM((ITERS, 2, 8) + tile, F32),
                pltpu.VMEM((ITERS, 2, 3, 3) + tile, F32),
                pltpu.VMEM((ITERS, 2, 3) + tile, F32),
                pltpu.VMEM((ITERS, 2, 5) + tile, F32),
                pltpu.VMEM((2, 3, 3 * CORE, SIZE), F32),
                pltpu.VMEM((2,) + field, F32),
                pltpu.VMEM((SLOTS, 2) + field, F32),
                pltpu.VMEM((SLOTS, 2) + field, F32),
                pltpu.VMEM((SLOTS, 2) + field, F32),
                pltpu.VMEM((2, SLOTS, 2, 2 * SIZE, SIZE), F32),
                pltpu.SemaphoreType.DMA((ITERS, 2, COPIES)),
                pltpu.SemaphoreType.DMA((ITERS, 2, COPIES)),
                pltpu.SemaphoreType.DMA((7,)),
            ],
            compiler_params=pltpu.CompilerParams(
                collective_id=0, has_side_effects=True, vmem_limit_bytes=60 * 1024 * 1024
            ),
        )(
            transmission,
            probe_field,
            propagator_phase,
            jnp.swapaxes(scan_offsets, 2, 3),
            position_counts,
            intensities,
            jnp.asarray(tables),
        )

    return jax.shard_map(
        on_device,
        mesh=mesh,
        in_specs=(
            P(None, None, "ty", "tx"),
            P(),
            P(),
            P("ty", "tx", None, None),
            P("ty", "tx"),
            P("ty", "tx", None, None, None),
        ),
        out_specs=P(None, None, "ty", "tx"),
        check_vma=False,
    )
```

```python
import functools
import math

import jax
import jax.numpy as jnp
import numpy as np
from jax import lax
from jax.experimental import pallas as pl
from jax.experimental.pallas import tpu as pltpu
from jax.sharding import PartitionSpec as P

ITERS = 2
STEP = 0.003
SIZE = 128
CORE = 64
SLOTS = 6
F32 = jnp.float32
BF16 = jnp.bfloat16

UP, DOWN, OUT, PAIR, OUT_UP, OUT_DOWN, PAIR_UP, PAIR_DOWN = range(8)
ROW_UP, ROW_DOWN, ROW_OWN = range(3)
ROW_START = (0, 128, 64)
COL_OUT, COL_OWN, COL_PAIR = range(3)
ADD_PAIR, CORNER_UP, CORNER_DOWN, ADD_UP, ADD_DOWN, ADD_OUT, ADD_PAIR_OWN = range(7)
COPIES = 15


def dft_blocks():
    index = np.arange(SIZE)
    angle = 2.0 * math.pi / SIZE * ((index[:, None] * index[None, :]) % SIZE)
    re = np.cos(angle) / math.sqrt(SIZE)
    im = -np.sin(angle) / math.sqrt(SIZE)
    right = np.block([[re, im], [-im, re]])
    blocks = np.stack([right, right.T])
    high = blocks.astype(BF16)
    low = (blocks - high.astype(np.float64)).astype(BF16)
    return np.stack([high, low], axis=1)


def split(x):
    high = x.astype(BF16)
    return high, (x - high.astype(F32)).astype(BF16)


def dot(a, b):
    return jnp.dot(a, b, preferred_element_type=F32)


def from_right(fields, table):
    high, low = split(
        jnp.concatenate(
            [
                jnp.concatenate([fields[0], fields[1]], axis=1),
                jnp.concatenate([fields[2], fields[3]], axis=1),
            ],
            axis=0,
        )
    )
    out = dot(high, table[0]) + dot(low, table[0]) + dot(high, table[1])
    return out[:SIZE, :SIZE], out[:SIZE, SIZE:], out[SIZE:, :SIZE], out[SIZE:, SIZE:]


def from_left(fields, table):
    high, low = split(
        jnp.concatenate(
            [
                jnp.concatenate([fields[0], fields[2]], axis=1),
                jnp.concatenate([fields[1], fields[3]], axis=1),
            ],
            axis=0,
        )
    )
    out = dot(table[0], high) + dot(table[0], low) + dot(table[1], high)
    return out[:SIZE, :SIZE], out[SIZE:, :SIZE], out[:SIZE, SIZE:], out[SIZE:, SIZE:]


def times(a, b):
    return a[0] * b[0] - a[1] * b[1], a[0] * b[1] + a[1] * b[0]


def times_conj(a, b):
    return a[0] * b[0] + a[1] * b[1], a[1] * b[0] - a[0] * b[1]


def lanes_of(shape):
    return lax.broadcasted_iota(jnp.int32, shape, 1)


def load_window(ext, offs, slice_, slot):
    row, col = offs[0, 0, 0, slot], offs[0, 0, 1, slot]
    rows = pl.ds(row, SIZE)
    back = lax.rem(SIZE - col, SIZE)
    keep = lanes_of((SIZE, SIZE)) < SIZE - col
    last = ext[slice_, 2, rows, :]
    re = jnp.where(
        keep, pltpu.roll(ext[slice_, 0, rows, :], back, 1), pltpu.roll(last, back, 1)
    )
    im = jnp.where(
        keep, pltpu.roll(ext[slice_, 1, rows, :], back, 1), pltpu.roll(last, CORE - col, 1)
    )
    return re, im


def store_field(padded, offs, slot, field):
    col = offs[0, 0, 1, slot]
    for part in range(2):
        padded[slot, part, CORE : CORE + SIZE, :] = pltpu.roll(field[part], col, 1)


def gradient_rows(padded, offs, start):
    lane = lanes_of((CORE, SIZE))
    sums = [jnp.zeros((CORE, SIZE), F32) for _ in range(4)]
    for slot in range(SLOTS):
        row, col = offs[0, 0, 0, slot], offs[0, 0, 1, slot]
        rows = pl.ds(CORE + start - row, CORE)
        here = lane >= col
        for part in range(2):
            value = padded[slot, part, rows, :]
            sums[part] = sums[part] + jnp.where(here, value, 0.0)
            sums[2 + part] = sums[2 + part] + jnp.where(here, 0.0, value)
    low = lane < CORE
    first = jnp.where(low, sums[0], pltpu.roll(sums[1], CORE, 1))
    second = jnp.where(low, pltpu.roll(sums[0], CORE, 1), sums[1])
    third = jnp.where(low, sums[2], pltpu.roll(sums[3], CORE, 1))
    return first, second, third


def transform(fields, tables, which, left_first=False):
    order = (from_left, from_right) if left_first else (from_right, from_left)
    for apply in order:
        fields = [apply(field, tables[which[0]] if apply is from_right else tables[which[1]]) for field in fields]
    return fields


FORWARD, INVERSE = (0, 1), (1, 0)
PAIRS = tuple((2 * pair, 2 * pair + 1) for pair in range(SLOTS // 2))


def forward_first(ext, offs, probe, prop, tables, psi):
    light = (probe[0], probe[1])
    fields = [
        times(light, load_window(ext, offs, 0, a)) + times(light, load_window(ext, offs, 0, b))
        for a, b in PAIRS
    ]
    fields = transform(fields, tables, FORWARD)
    factor = (prop[0], prop[1])
    fields = [times(field[:2], factor) + times(field[2:], factor) for field in fields]
    fields = transform(fields, tables, INVERSE, True)
    for slots, field in zip(PAIRS, fields):
        for n, slot in enumerate(slots):
            for part in range(2):
                psi[slot, part] = field[2 * n + part]


def middle(ext, offs, counts, measured, tables, psi, back, wins, padded):
    fields = []
    for slots in PAIRS:
        field = ()
        for slot in slots:
            window = load_window(ext, offs, 1, slot)
            wins[slot, 0] = window[0]
            wins[slot, 1] = window[1]
            field += times((psi[slot, 0], psi[slot, 1]), window)
        fields.append(field)
    fields = transform(fields, tables, FORWARD)
    grads = []
    for slots, field in zip(PAIRS, fields):
        grad = ()
        for n, slot in enumerate(slots):
            re, im = field[2 * n], field[2 * n + 1]
            live = jnp.where(slot < counts[0, 0], 4.0, 0.0)
            factor = live * (re * re + im * im - measured[0, 0, slot])
            grad += (factor * re, factor * im)
        grads.append(grad)
    grads = transform(grads, tables, INVERSE, True)
    for slots, both in zip(PAIRS, grads):
        for n, slot in enumerate(slots):
            grad = both[2 * n : 2 * n + 2]
            field = times_conj(grad, (wins[slot, 0], wins[slot, 1]))
            for part in range(2):
                back[slot, part] = field[part]
            store_field(
                padded, offs, slot, times_conj(grad, (psi[slot, 0], psi[slot, 1]))
            )


def backward_first(offs, probe, prop, tables, back, padded):
    fields = [
        (back[a, 0], back[a, 1], back[b, 0], back[b, 1]) for a, b in PAIRS
    ]
    fields = transform(fields, tables, FORWARD)
    factor = (prop[0], prop[1])
    fields = [times_conj(field[:2], factor) + times_conj(field[2:], factor) for field in fields]
    fields = transform(fields, tables, INVERSE, True)
    light = (probe[0], probe[1])
    for slots, field in zip(PAIRS, fields):
        for n, slot in enumerate(slots):
            store_field(
                padded, offs, slot, times_conj(field[2 * n : 2 * n + 2], light)
            )


def kernel(
    mesh_shape,
    obj_in,
    probe_in,
    phase_in,
    offs_in,
    counts_in,
    measured_in,
    tables_in,
    out,
    obj,
    probe,
    phase,
    offs,
    counts,
    measured,
    tables,
    own,
    halo,
    grads,
    passed,
    added,
    ext,
    prop,
    psi,
    back,
    wins,
    padded,
    send_sems,
    recv_sems,
    load_sems,
):
    ty_count, tx_count = mesh_shape
    row, col = lax.axis_index("ty"), lax.axis_index("tx")
    even = lax.rem(col, 2) == 0
    up = lax.rem(row + ty_count - 1, ty_count)
    down = lax.rem(row + 1, ty_count)
    right = lax.rem(col + 1, tx_count)
    left = lax.rem(col + tx_count - 1, tx_count)
    side = jnp.where(even, left, right)
    outer = {"ty": row, "tx": side}
    partner = {"ty": row, "tx": jnp.where(even, right, left)}
    above, below = {"ty": up, "tx": col}, {"ty": down, "tx": col}
    outer_above, outer_below = {"ty": up, "tx": side}, {"ty": down, "tx": side}
    has_above = row > 0
    has_below = row < ty_count - 1
    has_outer = jnp.logical_and(col > 0, col < tx_count - 1)

    barrier = pltpu.get_barrier_semaphore()
    for target in (outer, outer_above, outer_below, above, below, partner):
        pl.semaphore_signal(
            barrier, inc=1, device_id=target, device_id_type=pl.DeviceIdType.MESH
        )

    loads = [
        pltpu.make_async_copy(src, dst, load_sems.at[n])
        for n, (src, dst) in enumerate(
            (
                (obj_in, obj),
                (phase_in, phase),
                (offs_in, offs),
                (counts_in, counts),
                (probe_in, probe),
                (tables_in, tables),
                (measured_in, measured),
            )
        )
    ]
    for load in loads:
        load.start()

    low = lanes_of((CORE, SIZE)) < CORE
    loads[0].wait()
    for s in range(2):
        own[0, s] = jnp.concatenate([obj[0, s], obj[1, s]], axis=1)
    pl.semaphore_wait(barrier, 6)

    started = []

    def send(src, dst, step, s, kind, target):
        copy = pltpu.make_async_remote_copy(
            src_ref=src,
            dst_ref=dst,
            send_sem=send_sems.at[step, s, kind],
            recv_sem=recv_sems.at[step, s, kind],
            device_id=target,
            device_id_type=pl.DeviceIdType.MESH,
        )
        copy.start()
        started.append(copy)
        return copy

    def send_halo(step, s, kind, src, target):
        return send(src, halo.at[step, s, kind], step, s, kind, target)

    def halo_first(step, s):
        mine = own.at[step, s]
        return {
            kind: send_halo(step, s, kind, mine, target)
            for kind, target in (
                (DOWN, above),
                (UP, below),
                (OUT, outer),
                (OUT_DOWN, outer_above),
                (OUT_UP, outer_below),
                (PAIR, partner),
            )
        }

    def halo_second(step, s, copies):
        for kind, passed_on in ((UP, PAIR_UP), (DOWN, PAIR_DOWN)):
            copies[kind].wait_recv()
            copies[passed_on] = send_halo(
                step, s, passed_on, halo.at[step, s, kind], partner
            )

    def place(s, start, out_tile, own_tile, pair_tile):
        first = jnp.where(even, out_tile, pair_tile)
        third = jnp.where(even, pair_tile, out_tile)
        rows = slice(start, start + CORE)
        ext[s, 0, rows, :] = jnp.where(low, first, pltpu.roll(own_tile, CORE, 1))
        ext[s, 1, rows, :] = jnp.where(low, pltpu.roll(first, CORE, 1), own_tile)
        ext[s, 2, rows, :] = third

    def halo_last(step, s, copies):
        for kind in (PAIR, PAIR_UP, PAIR_DOWN, OUT_UP, OUT_DOWN, OUT):
            copies[kind].wait_recv()
        tile = lambda kind, ok: jnp.where(ok, halo[step, s, kind], 0.0)
        both = jnp.logical_and
        place(s, CORE, tile(OUT, has_outer), own[step, s], halo[step, s, PAIR])
        place(
            s,
            0,
            tile(OUT_UP, both(has_outer, has_above)),
            tile(UP, has_above),
            tile(PAIR_UP, has_above),
        )
        place(
            s,
            2 * CORE,
            tile(OUT_DOWN, both(has_outer, has_below)),
            tile(DOWN, has_below),
            tile(PAIR_DOWN, has_below),
        )

    def send_pair(step, s, copies, kind, tiles):
        copies[kind] = send(
            grads.at[step, s, COL_PAIR, tiles],
            passed.at[step, s, tiles],
            step,
            s,
            8 + kind,
            partner,
        )

    def reduce_first(step, s):
        sent = grads.at[step, s]
        copies = {}
        for tile, kind, target in (
            (ROW_UP, CORNER_DOWN, outer_above),
            (ROW_DOWN, CORNER_UP, outer_below),
            (ROW_OWN, ADD_OUT, outer),
        ):
            first, second, third = gradient_rows(padded.at[s], offs, ROW_START[tile])
            sent[COL_PAIR, tile] = jnp.where(even, third, first)
            if tile == ROW_DOWN:
                send_pair(step, s, copies, ADD_PAIR, pl.ds(ROW_UP, 2))
            sent[COL_OUT, tile] = jnp.where(even, first, third)
            copies[kind] = send(
                sent.at[COL_OUT, tile],
                added.at[step, s, kind - 1],
                step,
                s,
                8 + kind,
                target,
            )
            sent[COL_OWN, tile] = second
        send_pair(step, s, copies, ADD_PAIR_OWN, pl.ds(ROW_OWN, 1))
        return copies

    def masked(step, s, kind, ok):
        return jnp.where(ok, added[step, s, kind - 1], 0.0)

    def reduce_second(step, s, copies):
        mine = grads.at[step, s]
        copies[ADD_PAIR].wait_recv()
        for tile, kind, target in ((ROW_UP, ADD_DOWN, above), (ROW_DOWN, ADD_UP, below)):
            mine[COL_OWN, tile] = mine[COL_OWN, tile] + passed[step, s, tile]
            copies[kind] = send(
                mine.at[COL_OWN, tile],
                added.at[step, s, kind - 1],
                step,
                s,
                8 + kind,
                target,
            )

    def reduce_last(step, s, copies):
        copies[ADD_PAIR_OWN].wait_recv()
        total = grads[step, s, COL_OWN, ROW_OWN] + passed[step, s, ROW_OWN]
        both = jnp.logical_and
        for kind, ok in (
            (ADD_UP, has_above),
            (ADD_DOWN, has_below),
            (CORNER_UP, both(has_above, has_outer)),
            (CORNER_DOWN, both(has_below, has_outer)),
            (ADD_OUT, has_outer),
        ):
            copies[kind].wait_recv()
            total = total + masked(step, s, kind, ok)
        return own[step, s] - STEP * total

    first0 = halo_first(0, 0)
    first1 = halo_first(0, 1)
    loads[1].wait()
    prop[0] = jnp.cos(phase[...])
    prop[1] = jnp.sin(phase[...])
    zero = jnp.zeros((CORE, SIZE), F32)
    for s in range(2):
        for slot in range(SLOTS):
            for part in range(2):
                padded[s, slot, part, :CORE, :] = zero
                padded[s, slot, part, CORE + SIZE :, :] = zero

    for load in loads[2:]:
        load.wait()

    for step in range(ITERS):
        halo_second(step, 0, first0)
        halo_second(step, 1, first1)
        halo_last(step, 0, first0)
        forward_first(ext, offs, probe, prop, tables, psi)
        halo_last(step, 1, first1)
        middle(ext, offs, counts, measured, tables, psi, back, wins, padded.at[1])
        sums1 = reduce_first(step, 1)
        backward_first(offs, probe, prop, tables, back, padded.at[0])
        reduce_second(step, 1, sums1)
        sums0 = reduce_first(step, 0)
        reduce_second(step, 0, sums0)
        for s, sums in ((0, sums0), (1, sums1)):
            new = reduce_last(step, s, sums)
            if step < ITERS - 1:
                own[step + 1, s] = new
                copies = halo_first(step + 1, s)
                if s == 0:
                    first0 = copies
                else:
                    first1 = copies
            else:
                out[0, s] = new[:, :CORE]
                out[1, s] = pltpu.roll(new, CORE, 1)[:, :CORE]
    for copy in started:
        copy.wait_send()


def solution(mesh):
    shape = (mesh.shape["ty"], mesh.shape["tx"])
    vmem = pl.BlockSpec(memory_space=pltpu.VMEM)
    hbm = pl.BlockSpec(memory_space=pl.ANY)
    tables = dft_blocks()

    def on_device(
        transmission, probe_field, propagator_phase, scan_offsets, position_counts, intensities
    ):
        tile = (CORE, SIZE)
        field = (SIZE, SIZE)
        return pl.pallas_call(
            functools.partial(kernel, shape),
            out_shape=jax.ShapeDtypeStruct(transmission.shape, F32),
            in_specs=[hbm] * 7,
            out_specs=vmem,
            scratch_shapes=[
                pltpu.VMEM(transmission.shape, F32),
                pltpu.VMEM((2,) + field, F32),
                pltpu.VMEM(field, F32),
                pltpu.SMEM((1, 1, 2, SLOTS), jnp.int32),
                pltpu.SMEM((1, 1), jnp.int32),
                pltpu.VMEM(intensities.shape, F32),
                pltpu.VMEM(tables.shape, BF16),
                pltpu.VMEM((ITERS, 2) + tile, F32),
                pltpu.VMEM((ITERS, 2, 8) + tile, F32),
                pltpu.VMEM((ITERS, 2, 3, 3) + tile, F32),
                pltpu.VMEM((ITERS, 2, 3) + tile, F32),
                pltpu.VMEM((ITERS, 2, 5) + tile, F32),
                pltpu.VMEM((2, 3, 3 * CORE, SIZE), F32),
                pltpu.VMEM((2,) + field, F32),
                pltpu.VMEM((SLOTS, 2) + field, F32),
                pltpu.VMEM((SLOTS, 2) + field, F32),
                pltpu.VMEM((SLOTS, 2) + field, F32),
                pltpu.VMEM((2, SLOTS, 2, 2 * SIZE, SIZE), F32),
                pltpu.SemaphoreType.DMA((ITERS, 2, COPIES)),
                pltpu.SemaphoreType.DMA((ITERS, 2, COPIES)),
                pltpu.SemaphoreType.DMA((7,)),
            ],
            compiler_params=pltpu.CompilerParams(
                collective_id=0, has_side_effects=True, vmem_limit_bytes=60 * 1024 * 1024
            ),
        )(
            transmission,
            probe_field,
            propagator_phase,
            jnp.swapaxes(scan_offsets, 2, 3),
            position_counts,
            intensities,
            jnp.asarray(tables),
        )

    return jax.shard_map(
        on_device,
        mesh=mesh,
        in_specs=(
            P(None, None, "ty", "tx"),
            P(),
            P(),
            P("ty", "tx", None, None),
            P("ty", "tx"),
            P("ty", "tx", None, None, None),
        ),
        out_specs=P(None, None, "ty", "tx"),
        check_vma=False,
    )
```

```python
import functools
import math

import jax
import jax.numpy as jnp
import numpy as np
from jax import lax
from jax.experimental import pallas as pl
from jax.experimental.pallas import tpu as pltpu
from jax.sharding import PartitionSpec as P

ITERS = 2
STEP = 0.003
SIZE = 128
CORE = 64
SLOTS = 6
F32 = jnp.float32
BF16 = jnp.bfloat16

UP, DOWN, OUT, PAIR, OUT_UP, OUT_DOWN, PAIR_UP, PAIR_DOWN = range(8)
ROW_UP, ROW_DOWN, ROW_OWN = range(3)
ROW_START = (0, 128, 64)
COL_OUT, COL_OWN, COL_PAIR = range(3)
ADD_PAIR, CORNER_UP, CORNER_DOWN, ADD_UP, ADD_DOWN, ADD_OUT, ADD_PAIR_OWN = range(7)
COPIES = 15


def dft_blocks():
    index = np.arange(SIZE)
    angle = 2.0 * math.pi / SIZE * ((index[:, None] * index[None, :]) % SIZE)
    re = np.cos(angle) / math.sqrt(SIZE)
    im = -np.sin(angle) / math.sqrt(SIZE)
    right = np.block([[re, im], [-im, re]])
    blocks = np.stack([right, right.T])
    high = blocks.astype(BF16)
    low = (blocks - high.astype(np.float64)).astype(BF16)
    return np.stack([high, low], axis=1)


def split(x):
    high = x.astype(BF16)
    return high, (x - high.astype(F32)).astype(BF16)


def dot(a, b):
    return jnp.dot(a, b, preferred_element_type=F32)


def from_right(fields, table):
    high, low = split(
        jnp.concatenate(
            [
                jnp.concatenate([fields[0], fields[1]], axis=1),
                jnp.concatenate([fields[2], fields[3]], axis=1),
            ],
            axis=0,
        )
    )
    out = dot(high, table[0]) + dot(low, table[0]) + dot(high, table[1])
    return out[:SIZE, :SIZE], out[:SIZE, SIZE:], out[SIZE:, :SIZE], out[SIZE:, SIZE:]


def from_left(fields, table):
    high, low = split(
        jnp.concatenate(
            [
                jnp.concatenate([fields[0], fields[2]], axis=1),
                jnp.concatenate([fields[1], fields[3]], axis=1),
            ],
            axis=0,
        )
    )
    out = dot(table[0], high) + dot(table[0], low) + dot(table[1], high)
    return out[:SIZE, :SIZE], out[SIZE:, :SIZE], out[:SIZE, SIZE:], out[SIZE:, SIZE:]


def times(a, b):
    return a[0] * b[0] - a[1] * b[1], a[0] * b[1] + a[1] * b[0]


def times_conj(a, b):
    return a[0] * b[0] + a[1] * b[1], a[1] * b[0] - a[0] * b[1]


def lanes_of(shape):
    return lax.broadcasted_iota(jnp.int32, shape, 1)


def load_window(ext, offs, slice_, slot):
    row, col = offs[0, 0, 0, slot], offs[0, 0, 1, slot]
    rows = pl.ds(row, SIZE)
    back = lax.rem(SIZE - col, SIZE)
    keep = lanes_of((SIZE, SIZE)) < SIZE - col
    last = ext[slice_, 2, rows, :]
    re = jnp.where(
        keep, pltpu.roll(ext[slice_, 0, rows, :], back, 1), pltpu.roll(last, back, 1)
    )
    im = jnp.where(
        keep, pltpu.roll(ext[slice_, 1, rows, :], back, 1), pltpu.roll(last, CORE - col, 1)
    )
    return re, im


def store_field(padded, offs, slot, field):
    col = offs[0, 0, 1, slot]
    for part in range(2):
        padded[slot, part, CORE : CORE + SIZE, :] = pltpu.roll(field[part], col, 1)


def gradient_rows(padded, offs, start):
    lane = lanes_of((CORE, SIZE))
    sums = [jnp.zeros((CORE, SIZE), F32) for _ in range(4)]
    for slot in range(SLOTS):
        row, col = offs[0, 0, 0, slot], offs[0, 0, 1, slot]
        rows = pl.ds(CORE + start - row, CORE)
        here = lane >= col
        for part in range(2):
            value = padded[slot, part, rows, :]
            sums[part] = sums[part] + jnp.where(here, value, 0.0)
            sums[2 + part] = sums[2 + part] + jnp.where(here, 0.0, value)
    low = lane < CORE
    first = jnp.where(low, sums[0], pltpu.roll(sums[1], CORE, 1))
    second = jnp.where(low, pltpu.roll(sums[0], CORE, 1), sums[1])
    third = jnp.where(low, sums[2], pltpu.roll(sums[3], CORE, 1))
    return first, second, third


def transform(fields, tables, which, left_first=False):
    order = (from_left, from_right) if left_first else (from_right, from_left)
    for apply in order:
        fields = [apply(field, tables[which[0]] if apply is from_right else tables[which[1]]) for field in fields]
    return fields


FORWARD, INVERSE = (0, 1), (1, 0)
PAIRS = tuple((2 * pair, 2 * pair + 1) for pair in range(SLOTS // 2))


def forward_first(ext, offs, probe, prop, tables, psi):
    light = (probe[0], probe[1])
    fields = [
        times(light, load_window(ext, offs, 0, a)) + times(light, load_window(ext, offs, 0, b))
        for a, b in PAIRS
    ]
    fields = transform(fields, tables, FORWARD)
    factor = (prop[0], prop[1])
    fields = [times(field[:2], factor) + times(field[2:], factor) for field in fields]
    fields = transform(fields, tables, INVERSE, True)
    for slots, field in zip(PAIRS, fields):
        for n, slot in enumerate(slots):
            for part in range(2):
                psi[slot, part] = field[2 * n + part]


def middle(ext, offs, counts, measured, tables, psi, back, wins, padded):
    fields = []
    for slots in PAIRS:
        field = ()
        for slot in slots:
            window = load_window(ext, offs, 1, slot)
            wins[slot, 0] = window[0]
            wins[slot, 1] = window[1]
            field += times((psi[slot, 0], psi[slot, 1]), window)
        fields.append(field)
    fields = transform(fields, tables, FORWARD)
    grads = []
    for slots, field in zip(PAIRS, fields):
        grad = ()
        for n, slot in enumerate(slots):
            re, im = field[2 * n], field[2 * n + 1]
            live = jnp.where(slot < counts[0, 0], 4.0, 0.0)
            factor = live * (re * re + im * im - measured[0, 0, slot])
            grad += (factor * re, factor * im)
        grads.append(grad)
    grads = transform(grads, tables, INVERSE, True)
    for slots, both in zip(PAIRS, grads):
        for n, slot in enumerate(slots):
            grad = both[2 * n : 2 * n + 2]
            field = times_conj(grad, (wins[slot, 0], wins[slot, 1]))
            for part in range(2):
                back[slot, part] = field[part]
            store_field(
                padded, offs, slot, times_conj(grad, (psi[slot, 0], psi[slot, 1]))
            )


def backward_first(offs, probe, prop, tables, back, padded):
    fields = [
        (back[a, 0], back[a, 1], back[b, 0], back[b, 1]) for a, b in PAIRS
    ]
    fields = transform(fields, tables, FORWARD)
    factor = (prop[0], prop[1])
    fields = [times_conj(field[:2], factor) + times_conj(field[2:], factor) for field in fields]
    fields = transform(fields, tables, INVERSE, True)
    light = (probe[0], probe[1])
    for slots, field in zip(PAIRS, fields):
        for n, slot in enumerate(slots):
            store_field(
                padded, offs, slot, times_conj(field[2 * n : 2 * n + 2], light)
            )


def kernel(
    mesh_shape,
    obj_in,
    probe_in,
    phase_in,
    offs_in,
    counts_in,
    measured_in,
    tables_in,
    out,
    obj,
    probe,
    phase,
    offs,
    counts,
    measured,
    tables,
    own,
    halo,
    grads,
    passed,
    added,
    ext,
    prop,
    psi,
    back,
    wins,
    padded,
    send_sems,
    recv_sems,
    load_sems,
):
    ty_count, tx_count = mesh_shape
    row, col = lax.axis_index("ty"), lax.axis_index("tx")
    even = lax.rem(col, 2) == 0
    up = lax.rem(row + ty_count - 1, ty_count)
    down = lax.rem(row + 1, ty_count)
    right = lax.rem(col + 1, tx_count)
    left = lax.rem(col + tx_count - 1, tx_count)
    side = jnp.where(even, left, right)
    outer = {"ty": row, "tx": side}
    partner = {"ty": row, "tx": jnp.where(even, right, left)}
    above, below = {"ty": up, "tx": col}, {"ty": down, "tx": col}
    outer_above, outer_below = {"ty": up, "tx": side}, {"ty": down, "tx": side}
    has_above = row > 0
    has_below = row < ty_count - 1
    has_outer = jnp.logical_and(col > 0, col < tx_count - 1)

    barrier = pltpu.get_barrier_semaphore()
    for target in (outer, outer_above, outer_below, above, below, partner):
        pl.semaphore_signal(
            barrier, inc=1, device_id=target, device_id_type=pl.DeviceIdType.MESH
        )

    loads = [
        pltpu.make_async_copy(src, dst, load_sems.at[n])
        for n, (src, dst) in enumerate(
            (
                (obj_in, obj),
                (phase_in, phase),
                (offs_in, offs),
                (counts_in, counts),
                (probe_in, probe),
                (tables_in, tables),
                (measured_in, measured),
            )
        )
    ]
    for load in loads:
        load.start()

    low = lanes_of((CORE, SIZE)) < CORE
    loads[0].wait()
    for s in range(2):
        own[0, s] = jnp.concatenate([obj[0, s], obj[1, s]], axis=1)
    pl.semaphore_wait(barrier, 6)

    started = []

    def send(src, dst, step, s, kind, target):
        copy = pltpu.make_async_remote_copy(
            src_ref=src,
            dst_ref=dst,
            send_sem=send_sems.at[step, s, kind],
            recv_sem=recv_sems.at[step, s, kind],
            device_id=target,
            device_id_type=pl.DeviceIdType.MESH,
        )
        copy.start()
        started.append(copy)
        return copy

    def send_halo(step, s, kind, src, target):
        return send(src, halo.at[step, s, kind], step, s, kind, target)

    def halo_first(step, s):
        mine = own.at[step, s]
        return {
            kind: send_halo(step, s, kind, mine, target)
            for kind, target in (
                (DOWN, above),
                (UP, below),
                (OUT, outer),
                (OUT_DOWN, outer_above),
                (OUT_UP, outer_below),
                (PAIR, partner),
            )
        }

    def halo_second(step, s, copies):
        for kind, passed_on in ((UP, PAIR_UP), (DOWN, PAIR_DOWN)):
            copies[kind].wait_recv()
            copies[passed_on] = send_halo(
                step, s, passed_on, halo.at[step, s, kind], partner
            )

    def place(s, start, out_tile, own_tile, pair_tile):
        first = jnp.where(even, out_tile, pair_tile)
        third = jnp.where(even, pair_tile, out_tile)
        rows = slice(start, start + CORE)
        ext[s, 0, rows, :] = jnp.where(low, first, pltpu.roll(own_tile, CORE, 1))
        ext[s, 1, rows, :] = jnp.where(low, pltpu.roll(first, CORE, 1), own_tile)
        ext[s, 2, rows, :] = third

    def halo_last(step, s, copies):
        for kind in (PAIR, PAIR_UP, PAIR_DOWN, OUT_UP, OUT_DOWN, OUT):
            copies[kind].wait_recv()
        tile = lambda kind, ok: jnp.where(ok, halo[step, s, kind], 0.0)
        both = jnp.logical_and
        place(s, CORE, tile(OUT, has_outer), own[step, s], halo[step, s, PAIR])
        place(
            s,
            0,
            tile(OUT_UP, both(has_outer, has_above)),
            tile(UP, has_above),
            tile(PAIR_UP, has_above),
        )
        place(
            s,
            2 * CORE,
            tile(OUT_DOWN, both(has_outer, has_below)),
            tile(DOWN, has_below),
            tile(PAIR_DOWN, has_below),
        )

    def send_pair(step, s, copies, kind, tiles):
        copies[kind] = send(
            grads.at[step, s, COL_PAIR, tiles],
            passed.at[step, s, tiles],
            step,
            s,
            8 + kind,
            partner,
        )

    def reduce_first(step, s):
        sent = grads.at[step, s]
        copies, outward = {}, []
        for tile, kind, target in (
            (ROW_UP, CORNER_DOWN, outer_above),
            (ROW_DOWN, CORNER_UP, outer_below),
            (ROW_OWN, ADD_OUT, outer),
        ):
            first, second, third = gradient_rows(padded.at[s], offs, ROW_START[tile])
            sent[COL_PAIR, tile] = jnp.where(even, third, first)
            if tile == ROW_DOWN:
                send_pair(step, s, copies, ADD_PAIR, pl.ds(ROW_UP, 2))
            sent[COL_OUT, tile] = jnp.where(even, first, third)
            outward.append((kind, tile, target))
            sent[COL_OWN, tile] = second
        for kind, tile, target in outward[::-1]:
            copies[kind] = send(
                sent.at[COL_OUT, tile],
                added.at[step, s, kind - 1],
                step,
                s,
                8 + kind,
                target,
            )
        send_pair(step, s, copies, ADD_PAIR_OWN, pl.ds(ROW_OWN, 1))
        return copies

    def masked(step, s, kind, ok):
        return jnp.where(ok, added[step, s, kind - 1], 0.0)

    def reduce_second(step, s, copies):
        mine = grads.at[step, s]
        copies[ADD_PAIR].wait_recv()
        for tile, kind, target in ((ROW_UP, ADD_DOWN, above), (ROW_DOWN, ADD_UP, below)):
            mine[COL_OWN, tile] = mine[COL_OWN, tile] + passed[step, s, tile]
            copies[kind] = send(
                mine.at[COL_OWN, tile],
                added.at[step, s, kind - 1],
                step,
                s,
                8 + kind,
                target,
            )

    def reduce_last(step, s, copies):
        copies[ADD_PAIR_OWN].wait_recv()
        total = grads[step, s, COL_OWN, ROW_OWN] + passed[step, s, ROW_OWN]
        both = jnp.logical_and
        for kind, ok in (
            (ADD_UP, has_above),
            (ADD_DOWN, has_below),
            (CORNER_UP, both(has_above, has_outer)),
            (CORNER_DOWN, both(has_below, has_outer)),
            (ADD_OUT, has_outer),
        ):
            copies[kind].wait_recv()
            total = total + masked(step, s, kind, ok)
        return own[step, s] - STEP * total

    first0 = halo_first(0, 0)
    first1 = halo_first(0, 1)
    loads[1].wait()
    prop[0] = jnp.cos(phase[...])
    prop[1] = jnp.sin(phase[...])
    zero = jnp.zeros((CORE, SIZE), F32)
    for s in range(2):
        for slot in range(SLOTS):
            for part in range(2):
                padded[s, slot, part, :CORE, :] = zero
                padded[s, slot, part, CORE + SIZE :, :] = zero

    for load in loads[2:]:
        load.wait()

    for step in range(ITERS):
        halo_second(step, 0, first0)
        halo_second(step, 1, first1)
        halo_last(step, 0, first0)
        forward_first(ext, offs, probe, prop, tables, psi)
        halo_last(step, 1, first1)
        middle(ext, offs, counts, measured, tables, psi, back, wins, padded.at[1])
        sums1 = reduce_first(step, 1)
        backward_first(offs, probe, prop, tables, back, padded.at[0])
        reduce_second(step, 1, sums1)
        sums0 = reduce_first(step, 0)
        reduce_second(step, 0, sums0)
        for s, sums in ((0, sums0), (1, sums1)):
            new = reduce_last(step, s, sums)
            if step < ITERS - 1:
                own[step + 1, s] = new
                copies = halo_first(step + 1, s)
                if s == 0:
                    first0 = copies
                else:
                    first1 = copies
            else:
                out[0, s] = new[:, :CORE]
                out[1, s] = pltpu.roll(new, CORE, 1)[:, :CORE]
    for copy in started:
        copy.wait_send()


def solution(mesh):
    shape = (mesh.shape["ty"], mesh.shape["tx"])
    vmem = pl.BlockSpec(memory_space=pltpu.VMEM)
    hbm = pl.BlockSpec(memory_space=pl.ANY)
    tables = dft_blocks()

    def on_device(
        transmission, probe_field, propagator_phase, scan_offsets, position_counts, intensities
    ):
        tile = (CORE, SIZE)
        field = (SIZE, SIZE)
        return pl.pallas_call(
            functools.partial(kernel, shape),
            out_shape=jax.ShapeDtypeStruct(transmission.shape, F32),
            in_specs=[hbm] * 7,
            out_specs=vmem,
            scratch_shapes=[
                pltpu.VMEM(transmission.shape, F32),
                pltpu.VMEM((2,) + field, F32),
                pltpu.VMEM(field, F32),
                pltpu.SMEM((1, 1, 2, SLOTS), jnp.int32),
                pltpu.SMEM((1, 1), jnp.int32),
                pltpu.VMEM(intensities.shape, F32),
                pltpu.VMEM(tables.shape, BF16),
                pltpu.VMEM((ITERS, 2) + tile, F32),
                pltpu.VMEM((ITERS, 2, 8) + tile, F32),
                pltpu.VMEM((ITERS, 2, 3, 3) + tile, F32),
                pltpu.VMEM((ITERS, 2, 3) + tile, F32),
                pltpu.VMEM((ITERS, 2, 5) + tile, F32),
                pltpu.VMEM((2, 3, 3 * CORE, SIZE), F32),
                pltpu.VMEM((2,) + field, F32),
                pltpu.VMEM((SLOTS, 2) + field, F32),
                pltpu.VMEM((SLOTS, 2) + field, F32),
                pltpu.VMEM((SLOTS, 2) + field, F32),
                pltpu.VMEM((2, SLOTS, 2, 2 * SIZE, SIZE), F32),
                pltpu.SemaphoreType.DMA((ITERS, 2, COPIES)),
                pltpu.SemaphoreType.DMA((ITERS, 2, COPIES)),
                pltpu.SemaphoreType.DMA((7,)),
            ],
            compiler_params=pltpu.CompilerParams(
                collective_id=0, has_side_effects=True, vmem_limit_bytes=60 * 1024 * 1024
            ),
        )(
            transmission,
            probe_field,
            propagator_phase,
            jnp.swapaxes(scan_offsets, 2, 3),
            position_counts,
            intensities,
            jnp.asarray(tables),
        )

    return jax.shard_map(
        on_device,
        mesh=mesh,
        in_specs=(
            P(None, None, "ty", "tx"),
            P(),
            P(),
            P("ty", "tx", None, None),
            P("ty", "tx"),
            P("ty", "tx", None, None, None),
        ),
        out_specs=P(None, None, "ty", "tx"),
        check_vma=False,
    )
```
